128 devices in a mesh: gz: 8 (over x, core), gy: 4 (over y), gx: 4 (over z).
Axes of the slice: x: 4, y: 4, z: 4, core: 2. Of those that a mesh axis runs over, the one named last changes fastest.
Arguments:
- charges: float32 [512, 512, 512], P('gz', 'gy', 'gx'), may hold values from -6 to 6
- level_taps: float32 [3, 9], replicated, may hold values from -1 to 1
- top_taps: float32 [64], replicated, may hold values from -0.5 to 0.5
Outputs:
- potential: float32 [512, 512, 512], P('gz', 'gy', 'gx')
The draws below stay inside these ranges and needn't reach their ends.
All inputs are finite; a program needn't handle non-finite values.
Results may differ from the reference program's by a relative error of at most 0.00011.
Values sent between devices are 32-bit elements; how exact they have to be, the bound alone decides.
No kernel may reach another device: no remote copies, remote signals or barrier semaphores. Data moves between devices by JAX's collectives and lax.ppermute only.
A program may use at most 128 MiB of HBM per device.

```python
import jax
import jax.numpy as jnp
from jax import lax

LEVELS = 3
TAPS = 9
NZ = 512
NY = 512
NX = 512
TOPN = 64


def shard_levels(key, extent, shards, low, high):
    def one(dim, shards_of):
        heights = jax.random.uniform(jax.random.fold_in(jax.random.fold_in(key, 6), dim), (shards_of,), jnp.float32, low / len(shards), high / len(shards))
        return jnp.repeat(jnp.exp(heights), extent[dim] // shards_of).reshape((-1,) + (1,) * (len(extent) - dim - 1))

    factor_of = one(*shards[0])
    for cut in shards[1:]:
        factor_of = factor_of * one(*cut)
    return factor_of


def bell_draw(rng, dims, scale, reach, pieces=(), held_as=jnp.bfloat16):
    values = jax.random.normal(rng, dims, jnp.float32) * scale
    if len(pieces) > 0:
        values = shard_levels(rng, dims, pieces, -0.22, 0.18) * values
    return jnp.clip(values, min=-reach, max=reach).astype(held_as)


def setup_inputs(seed: int = 0) -> dict:
    arg_keys = jax.random.split(jax.random.key(seed), 4)
    charges = bell_draw(arg_keys[0], (NZ, NY, NX), 1.0, 6.0, ((0, 8), (1, 4), (2, 4)), jnp.float32)
    level_taps = bell_draw(arg_keys[1], (LEVELS, TAPS), 0.25, 1.0, (), jnp.float32)
    top_taps = bell_draw(arg_keys[2], (TOPN,), 0.125, 0.5, (), jnp.float32)
    return {"charges": charges, "level_taps": level_taps, "top_taps": top_taps}


def smooth(field, taps, axis):
    size = field.shape[axis]
    widths = [(0, 0), (0, 0), (0, 0)]
    widths[axis] = (8, 8)
    padded = jnp.pad(field, widths)
    total = taps[0] * field
    for dist in range(1, 9):
        upper = lax.slice_in_dim(padded, 8 + dist, 8 + dist + size, 1, axis)
        lower = lax.slice_in_dim(padded, 8 - dist, 8 - dist + size, 1, axis)
        total = total + taps[dist] * (upper + lower)
    return total


def restrict(field, axis):
    size = field.shape[axis]
    widths = [(0, 0), (0, 0), (0, 0)]
    widths[axis] = (3, 3)
    padded = jnp.pad(field, widths)

    def pick(offset):
        return lax.slice_in_dim(padded, 3 + offset, 3 + offset + size - 1, 2, axis)

    return pick(0) + 0.5625 * (pick(-1) + pick(1)) - 0.0625 * (pick(-3) + pick(3))


def prolong(field, axis):
    size = field.shape[axis]
    widths = [(0, 0), (0, 0), (0, 0)]
    widths[axis] = (2, 2)
    padded = jnp.pad(field, widths)

    def pick(offset):
        return lax.slice_in_dim(padded, 2 + offset, 2 + offset + size, 1, axis)

    odd = 0.5625 * (pick(0) + pick(1)) - 0.0625 * (pick(-1) + pick(2))
    joined = jnp.stack([field, odd], axis=axis + 1)
    shape = list(field.shape)
    shape[axis] = 2 * size
    return joined.reshape(shape)


def toeplitz(taps, size):
    dist = jnp.abs(jnp.arange(size)[:, None] - jnp.arange(size)[None, :])
    return taps[dist]


def reference(charges, level_taps, top_taps):
    grids = [charges]
    for level in range(LEVELS):
        field = grids[-1]
        for axis in (2, 1, 0):
            field = restrict(field, axis)
        grids.append(field)
    top = grids[LEVELS]
    high = lax.Precision.HIGHEST
    top = jnp.einsum("zye,ex->zyx", top, toeplitz(top_taps, top.shape[2]), precision=high)
    top = jnp.einsum("zex,ey->zyx", top, toeplitz(top_taps, top.shape[1]), precision=high)
    top = jnp.einsum("eyx,ez->zyx", top, toeplitz(top_taps, top.shape[0]), precision=high)
    result = top * 0.125
    for level in range(LEVELS - 1, -1, -1):
        near = grids[level]
        for axis in (2, 1, 0):
            near = smooth(near, level_taps[level], axis)
        coarse = result
        for axis in (2, 1, 0):
            coarse = prolong(coarse, axis)
        result = near * (2.0 ** (-level)) + coarse
    return result
```

```python
import jax
import jax.numpy as jnp
import numpy as np
from jax import lax
from jax.sharding import PartitionSpec as P

AXES = ("gz", "gy", "gx")
FORMS = ("zyx,az->ayx", "zyx,ay->zax", "zyx,ax->zya")


def phi(dist):
    dist = np.abs(dist)
    return np.where(
        dist == 0, 1.0, np.where(dist == 1, 0.5625, np.where(dist == 3, -0.0625, 0.0))
    )


def restrict_whole(size):
    rows = np.arange(size // 2)[:, None]
    cols = np.arange(size)[None, :]
    return phi(cols - 2 * rows)


def rows_of(whole, first, count):
    picked = np.zeros((count, whole.shape[1]))
    for r in range(count):
        if 0 <= first + r < whole.shape[0]:
            picked[r] = whole[first + r]
    return picked


def chain_tables(size, count):
    own0 = size // count
    first = restrict_whole(size)
    second = restrict_whole(size // 2) @ first
    tables = []
    for whole, own, low, high in ((first, own0 // 2, 1, 2), (second, own0 // 4, 2, 3)):
        stack = []
        for place in range(count):
            cols = whole[:, place * own0 : (place + 1) * own0]
            stack.append(rows_of(cols, place * own - low, own + low + high))
        tables.append(np.stack(stack).astype(np.float32))
    return tables


def prolong_tables(size, count):
    tables = []
    for level, (low, high, from_low, from_high) in (
        (2, (2, 3, 2, 3)),
        (1, (1, 2, 2, 3)),
        (0, (0, 0, 1, 2)),
    ):
        total = size >> level
        own = total // count
        stack = []
        for place in range(count):
            i = np.arange(-low, own + high)[:, None]
            coarse = np.arange(-from_low, own // 2 + from_high)[None, :]
            table = phi(i - 2 * coarse)
            where = i + place * own
            stack.append(table * ((where >= 0) & (where < total)))
        tables.append(np.stack(stack).astype(np.float32))
    return tables


def pick(tables, place):
    return lax.dynamic_index_in_dim(jnp.asarray(tables), place, 0, keepdims=False)


def band(taps, out_rows, in_count):
    dist = np.abs(np.asarray(out_rows)[:, None] - np.arange(in_count)[None, :])
    hot = (dist[:, :, None] == np.arange(9)).astype(np.float32)
    return jnp.sum(jnp.asarray(hot) * taps, axis=-1)


def apply(field, matrix, axis, precision=lax.Precision.HIGH):
    return jnp.einsum(FORMS[axis], field, matrix, precision=precision)


def shift(value, name, step):
    count = lax.axis_size(name)
    return lax.ppermute(value, name, [(i, (i + step) % count) for i in range(count)])


def cut(field, axis, first, count):
    return lax.slice_in_dim(field, first, first + count, axis=axis)


def add_edges(own, from_low, from_high, axis):
    size = own.shape[axis]

    def widen(part, before):
        widths = [(0, 0)] * 3
        widths[axis] = (before, size - before - part.shape[axis])
        return jnp.pad(part, widths)

    return own + widen(from_low, 0) + widen(from_high, size - from_high.shape[axis])


def chain_pass(field, table, axis, low, high):
    name = AXES[axis]
    full = apply(field, table, axis)
    own = full.shape[axis] - low - high
    to_low = cut(full, axis, 0, low)
    to_high = cut(full, axis, low + own, high)
    from_high = shift(to_low, name, -1)
    from_low = shift(to_high, name, 1)
    return add_edges(cut(full, axis, low, own), from_low, from_high, axis)


def near_pass(field, taps, axis, low, high, factor=1.0):
    name = AXES[axis]
    place = lax.axis_index(name)
    count = lax.axis_size(name)
    own = field.shape[axis]
    mine = np.arange(-low, own + high)
    down = np.arange(-8, high)
    up = np.arange(own - low, own + 8)
    matrix = band(taps, np.concatenate([mine, down, up]), own) * factor
    where = jnp.asarray(mine) + place * own
    keep = jnp.concatenate(
        [
            (where >= 0) & (where < own * count),
            jnp.broadcast_to(place > 0, down.shape),
            jnp.broadcast_to(place < count - 1, up.shape),
        ]
    )
    matrix = jnp.where(keep[:, None], matrix, 0.0)
    full = apply(field, matrix, axis)
    to_low = cut(full, axis, mine.size, down.size)
    to_high = cut(full, axis, mine.size + down.size, up.size)
    from_high = shift(to_low, name, -1)
    from_low = shift(to_high, name, 1)
    return add_edges(cut(full, axis, 0, mine.size), from_low, from_high, axis)


def top_matrix(top_taps, axis, own, count, place):
    size3 = own * count // 2
    own3 = own // 2
    where = np.concatenate([p * own3 + np.arange(-2, own3 + 3) for p in range(count)])
    ok = ((where >= 0) & (where < size3)).astype(np.float32)
    dist = np.clip(np.abs(where[:, None] - np.arange(size3)[None, :]), 0, size3 - 1)
    hot = (dist[:, :, None] == np.arange(size3)).astype(np.float32) * ok[:, None, None]
    kernel = jnp.sum(jnp.asarray(hot) * top_taps, axis=-1)
    whole = restrict_whole(own * count).astype(np.float32)
    cols = lax.dynamic_slice_in_dim(jnp.asarray(whole), place * own, own, axis=1)
    return jnp.dot(kernel, cols, precision=lax.Precision.HIGHEST)


def top_pass(field, top_taps, axis, factor=1.0):
    name = AXES[axis]
    place = lax.axis_index(name)
    count = lax.axis_size(name)
    own = field.shape[axis]
    rows = own // 2 + 5
    matrix = top_matrix(top_taps, axis, own, count, place) * factor
    matrix = matrix.reshape(count, rows, own)
    total = None
    for step in range(count):
        target = lax.rem(place + step, count)
        part = apply(field, lax.dynamic_index_in_dim(matrix, target, 0, False), axis)
        if step:
            part = shift(part, name, step)
        total = part if total is None else total + part
    return total


def per_device(charges, level_taps, top_taps):
    sizes = [charges.shape[a] * lax.axis_size(AXES[a]) for a in range(3)]
    places = [lax.axis_index(name) for name in AXES]
    g1 = charges
    g2 = charges
    for axis in (0, 1, 2):
        first, second = chain_tables(sizes[axis], lax.axis_size(AXES[axis]))
        g1 = chain_pass(g1, pick(first, places[axis]), axis, 1, 2)
        g2 = chain_pass(g2, pick(second, places[axis]), axis, 2, 3)
    near0, near1, near2, top = charges, g1, g2, g2
    for axis in (0, 1, 2):
        last = axis == 2
        top = top_pass(top, top_taps, axis, 0.125 if last else 1.0)
        near2 = near_pass(near2, level_taps[2], axis, 2, 3, 0.25 if last else 1.0)
        near1 = near_pass(near1, level_taps[1], axis, 1, 2, 0.5 if last else 1.0)
        near0 = near_pass(near0, level_taps[0], axis, 0, 0)
    ups = [prolong_tables(sizes[a], lax.axis_size(AXES[a])) for a in range(3)]
    result = top
    for step, near in enumerate((near2, near1, near0)):
        for axis in (2, 1, 0):
            result = apply(result, pick(ups[axis][step], places[axis]), axis)
        result = result + near
    return result


def solution(mesh):
    return jax.shard_map(
        per_device,
        mesh=mesh,
        in_specs=(P("gz", "gy", "gx"), P(), P()),
        out_specs=P("gz", "gy", "gx"),
        check_vma=False,
    )
```

```python
import jax
import jax.numpy as jnp
import numpy as np
from jax import lax
from jax.experimental import pallas as pl
from jax.experimental.pallas import tpu as pltpu
from jax.sharding import PartitionSpec as P

AXES = ("gz", "gy", "gx")
F32 = jnp.float32
BF16 = jnp.bfloat16
NN = (((1,), (0,)), ((), ()))
NT = (((1,), (1,)), ((), ()))
ANY = pl.BlockSpec(memory_space=pl.ANY)
SMEM = pl.BlockSpec(memory_space=pltpu.SMEM)
VMEM = pl.BlockSpec(memory_space=pltpu.VMEM)


def phi(dist):
    dist = np.abs(dist)
    return np.where(
        dist == 0, 1.0, np.where(dist == 1, 0.5625, np.where(dist == 3, -0.0625, 0.0))
    )


def restrict_whole(size):
    rows = np.arange(size // 2)[:, None]
    cols = np.arange(size)[None, :]
    return phi(cols - 2 * rows)


def rows_of(whole, first, count):
    picked = np.zeros((count, whole.shape[1]))
    for r in range(count):
        if 0 <= first + r < whole.shape[0]:
            picked[r] = whole[first + r]
    return picked


def chain_tables(size, count):
    own0 = size // count
    first = restrict_whole(size)
    second = restrict_whole(size // 2) @ first
    stack = []
    for place in range(count):
        parts = []
        for whole, own, low, high in ((first, own0 // 2, 1, 2), (second, own0 // 4, 2, 3)):
            cols = whole[:, place * own0 : (place + 1) * own0]
            at = place * own
            parts.append(rows_of(cols, at, own))
            parts.append(np.zeros((8 - low, own0)))
            parts.append(rows_of(cols, at - low, low))
            parts.append(rows_of(cols, at + own, high))
            parts.append(np.zeros((8 - high, own0)))
        stack.append(np.concatenate(parts))
    return np.stack(stack).astype(jnp.bfloat16)


def prolong_table(total, count, low, high, from_low, from_high, shape):
    own = total // count
    stack = []
    for place in range(count):
        i = np.arange(-low, own + high)[:, None]
        coarse = np.arange(-from_low, own // 2 + from_high)[None, :]
        where = i + place * own
        table = phi(i - 2 * coarse) * ((where >= 0) & (where < total))
        whole = np.zeros(shape)
        whole[: table.shape[0], : table.shape[1]] = table
        stack.append(whole)
    return np.stack(stack)


def shift(value, name, step):
    count = lax.axis_size(name)
    return lax.ppermute(value, name, [(i, (i + step) % count) for i in range(count)])


def split(x):
    high = x.astype(BF16)
    return high, (x - high.astype(F32)).astype(BF16)


def dot(a, b, dims=NN):
    return lax.dot_general(a, b, dims, preferred_element_type=F32)


def mm(a, b):
    a_high, a_low = split(a)
    b_high, b_low = split(b)
    return dot(a_high, b_high) + (dot(a_low, b_high) + dot(a_high, b_low))


def exact_left(table, x):
    high, low = split(x)
    return dot(table, high) + dot(table, low)


def exact_right(x, table):
    high, low = split(x)
    return dot(high, table) + dot(low, table)


def neighbours(name):
    place = lax.axis_index(name)
    count = lax.axis_size(name)
    return (place > 0).astype(F32), (place < count - 1).astype(F32)


def call(body, outs, cost=0, vmem=16, **kwargs):
    shapes = [jax.ShapeDtypeStruct(s, F32) for s in outs]
    return pl.pallas_call(
        body,
        out_shape=shapes,
        compiler_params=pltpu.CompilerParams(vmem_limit_bytes=vmem * 1024 * 1024),
        cost_estimate=pl.CostEstimate(flops=cost, bytes_accessed=8 << 20, transcendentals=0),
        **kwargs,
    )


def coarse_z_body(g, own1, own2, low, high):
    has_low, has_high = neighbours("gz")
    for chunk in range(g.shape[1] // 8):
        rows = pl.ds(8 * chunk, 8)

        def weigh(at, count, get, low_at=0):
            total = None
            for offsets, weight in (((0,), 1.0), ((-1, 1), 0.5625), ((-3, 3), -0.0625)):
                part = None
                for o in offsets:
                    if low_at <= 2 * at + o < count:
                        value = get(2 * at + o)
                        part = value if part is None else part + value
                if part is not None:
                    part = part if weight == 1.0 else part * weight
                    total = part if total is None else total + part
            return total

        planes = {}

        def get(i):
            if i not in planes:
                planes[i] = g[i, rows, :]
            return planes[i]

        first = {}
        for j in range(-1, 34):
            first[j] = weigh(j, 64, get)
            if 0 <= j < 32:
                own1[j, rows, :] = first[j]
        for j, has in ((-1, has_low), (32, has_high), (33, has_high)):
            first[j] = first[j] * has
        low[0, rows, :] = first[-1]
        high[0, rows, :] = first[32]
        high[1, rows, :] = first[33]
        for k in range(-2, 19):
            value = weigh(k, 34, lambda j: first[j], -1)
            if k < 0:
                low[3 + k, rows, :] = value * has_low
            elif k < 16:
                own2[k, rows, :] = value
            else:
                high[k - 14, rows, :] = value * has_high


def coarse_z(g):
    block = lambda n: pl.BlockSpec((n, 32, 128), lambda i: (0, i, 0))
    return call(
        coarse_z_body,
        [(32, 128, 128), (16, 128, 128), (3, 128, 128), (5, 128, 128)],
        cost=6 << 20,
        grid=(4,),
        in_specs=[block(64)],
        out_specs=[block(32), block(16), block(3), block(5)],
    )(g)


def coarse_x_body(table, own1, own2, from_high, from_low, out1, out2, low, high):
    step = pl.program_id(0)
    own_table = table[lax.axis_index("gx")]
    doubled = jnp.concatenate([own_table, own_table], axis=1)

    def planes(source, extra):
        values = [source[k] for k in range(8)]
        for k, part in extra:
            values[k] = values[k] + part
        return values

    def work(values, first, rows, out):
        for pair in range(4):
            both = jnp.concatenate([values[2 * pair], values[2 * pair + 1]], axis=0)
            wide = jnp.concatenate(split(both), axis=1)
            full = dot(doubled[first : first + rows + 16], wide, NT)
            for k in range(2):
                part = full[:, 128 * k : 128 * k + 128]
                at = 2 * pair + k
                out[at] = part[:rows]
                low[at] = part[rows : rows + 8]
                high[at] = part[rows + 8 :]

    @pl.when(step == 0)
    def _():
        work(planes(own1, [(0, from_low[0]), (1, from_low[1])]), 0, 64, out1)

    @pl.when((step == 1) | (step == 2))
    def _():
        work(planes(own1, []), 0, 64, out1)

    @pl.when(step == 3)
    def _():
        work(planes(own1, [(7, from_high[0])]), 0, 64, out1)

    @pl.when(step == 4)
    def _():
        extra = [(0, from_low[2]), (1, from_low[3]), (2, from_low[4])]
        work(planes(own2, extra), 80, 32, out2)

    @pl.when(step == 5)
    def _():
        work(planes(own2, [(6, from_high[1]), (7, from_high[2])]), 80, 32, out2)


def coarse_x(table, own1, own2, from_high, from_low):
    early = lambda n: pl.BlockSpec((8, n, 128), lambda i: (jnp.minimum(i, 3), 0, 0))
    late = lambda n: pl.BlockSpec((8, n, 128), lambda i: (jnp.maximum(i - 4, 0), 0, 0))
    each = pl.BlockSpec((8, 8, 128), lambda i: (i, 0, 0))
    return call(
        coarse_x_body,
        [(32, 64, 128), (16, 32, 128), (48, 8, 128), (48, 8, 128)],
        cost=600 << 20,
        grid=(6,),
        in_specs=[VMEM, early(128), late(128), VMEM, VMEM],
        out_specs=[early(64), late(32), each, each],
    )(table, own1, own2, from_high, from_low)


def coarse_y_body(table, own1, own2, from_high, from_low, out1, out2, low, high):
    own_table = table[lax.axis_index("gy")]
    doubled = jnp.concatenate([own_table, own_table], axis=1)
    for source, base, first, rows, each, out, at in (
        (own1, 0, 0, 64, 4, out1, 0),
        (own2, 32, 80, 32, 8, out2, 2048),
    ):
        for group in range(source.shape[0] // each):
            parts = []
            for k in range(each):
                z = group * each + k
                parts.append(source[z, 0:8] + from_low[base + z])
                parts.append(source[z, 8 : rows - 8])
                parts.append(source[z, rows - 8 : rows] + from_high[base + z])
            wide = jnp.concatenate(split(jnp.concatenate(parts, axis=0)), axis=1)
            full = dot(doubled[first : first + rows + 16], wide, NT)
            lanes = pl.ds(256 * group, 256)
            out[:, lanes] = full[:rows]
            lanes = pl.ds(at + 256 * group, 256)
            low[:, lanes] = full[rows : rows + 8]
            high[:, lanes] = full[rows + 8 :]


def coarse_y(table, own1, own2, from_high, from_low):
    return call(
        coarse_y_body,
        [(64, 2048), (32, 512), (8, 2560), (8, 2560)],
        cost=300 << 20,
        in_specs=[VMEM] * 5,
        out_specs=[VMEM] * 4,
    )(table, own1, own2, from_high, from_low)


def top_y_body(table, own2, from_high, from_low, top, near, up, down, far):
    fh, fl = from_high[:, 2048:], from_low[:, 2048:]
    value = jnp.concatenate(
        [own2[0:8] + fl, own2[8:24], own2[24:32] + fh], axis=0
    )
    full = mm(table[...], value)
    top[...] = full[0:24]
    up[0:24] = full[24:48]
    far[...] = full[48:72]
    down[0:24] = full[72:96]
    near[...] = full[96:136]
    down[24:40] = full[136:152]
    up[24:40] = full[152:168]


def top_y(table, own2, from_high, from_low):
    return call(
        top_y_body,
        [(24, 512), (40, 512), (40, 512), (40, 512), (24, 512)],
        cost=50 << 20,
        in_specs=[VMEM] * 4,
        out_specs=[VMEM] * 5,
    )(table, own2, from_high, from_low)


def top_x_body(ttable, ntable, top, near, f_low, f_high, f_far, otop, onear, up, down, far):
    total = top[...] + f_low[0:24] + (f_high[0:24] + f_far[...])
    extended = jnp.concatenate(
        [near[0:16] + f_low[24:40], near[16:24], near[24:40] + f_high[24:40]], axis=0
    )
    stacked = jnp.concatenate([total[:, 128 * t : 128 * t + 128] for t in range(4)], axis=0)
    full = mm(stacked, ttable[...])
    otop[...] = full[:, 0:128]
    up[0:96] = full[:, 128:256]
    far[...] = full[:, 256:384]
    down[0:96] = full[:, 384:512]
    stacked = jnp.concatenate([extended[:, 128 * t : 128 * t + 128] for t in range(4)], axis=0)
    full = mm(stacked, ntable[...])
    onear[...] = full[:, 0:256]
    down[96:256] = full[:, 256:384]
    up[96:256] = full[:, 384:512]


def top_x(ttable, ntable, top, near, f_low, f_high, f_far):
    return call(
        top_x_body,
        [(96, 128), (160, 256), (256, 128), (256, 128), (96, 128)],
        cost=50 << 20,
        in_specs=[VMEM] * 7,
        out_specs=[VMEM] * 5,
    )(ttable, ntable, top, near, f_low, f_high, f_far)


def grid_of(rows, cols):
    shape = (rows, cols)
    return lax.broadcasted_iota(jnp.int32, shape, 0), lax.broadcasted_iota(jnp.int32, shape, 1)


def lane_of(rows):
    return lax.broadcasted_iota(jnp.int32, (rows, 128), 1)


def top_z_body(tcoef, ncoef, top, near, f_low, f_high, f_far, otop, onear, up, down, *others):
    total = top[...] + f_low[0:96] + (f_high[0:96] + f_far[...])
    group = lane_of(24) // 32
    planes = []
    for z in range(16):
        tile = total[24 * (z // 4) : 24 * (z // 4) + 24]
        part = jnp.where(group == z % 4, tile, 0.0)
        part = part + pltpu.roll(part, 32, 1)
        planes.append(part + pltpu.roll(part, 64, 1))
    outs = [otop, up, *others, down]
    for step in range(8):
        for quarter in range(4):
            value = None
            for z in range(16):
                at = (step * 4 + quarter) * 16 + z
                part = planes[z] * tcoef[at : at + 1, :]
                value = part if value is None else value + part
            outs[step][24 * quarter : 24 * quarter + 24] = value
    lane = lane_of(40)
    planes = []
    for z in range(16):
        tile, q = z // 4, z % 4
        rows = slice(40 * tile, 40 * tile + 40)
        part = near[rows, 128 * (q // 2) : 128 * (q // 2) + 128]
        part = jnp.where(lane // 64 == q % 2, part, 0.0)
        low = jnp.where(lane // 32 == q, f_low[96 + 40 * tile : 136 + 40 * tile], 0.0)
        high = jnp.where(lane // 32 == q, f_high[96 + 40 * tile : 136 + 40 * tile], 0.0)
        if q % 2:
            part = pltpu.roll(part, 64, 1)
        if q:
            low = pltpu.roll(low, 128 - 32 * q, 1)
        high = pltpu.roll(high, (26 - 32 * q) % 128, 1)
        part = part + (low + high)
        planes.append(part + pltpu.roll(part, 64, 1))
    for out, base, count, first, offset in ((onear, 0, 11, -2, 0), (down, 11, 6, -8, 96), (up, 17, 5, 14, 96)):
        for p in range(count):
            value = None
            for z in range(16):
                r = first + 2 * p
                if min(abs(r - z), abs(r + 1 - z)) > 8:
                    continue
                at = (base + p) * 16 + z
                part = planes[z] * ncoef[at : at + 1, :]
                value = part if value is None else value + part
            out[offset + 40 * p : offset + 40 * p + 40] = value


def top_z(tcoef, ncoef, top, near, f_low, f_high, f_far):
    return call(
        top_z_body,
        [(96, 128), (440, 128), (296, 128), (336, 128)] + [(96, 128)] * 5,
        cost=50 << 20,
        in_specs=[VMEM] * 7,
        out_specs=[VMEM] * 9,
    )(tcoef, ncoef, top, near, f_low, f_high, f_far)


def rise_body(py2, px2, mask2, py1, px1, mask1, py0, px0, top, near2, f_low, f_high, *rest):
    others, (near1, n_low, n_high, out, middle) = rest[:5], rest[5:]
    z, y, x = [lax.axis_index(name) for name in AXES]
    py2, py1, py0 = py2[y], py1[y], py0[y]
    px2, px1, px0 = px2[x], px1[x], px0[x]
    total = top[...] + f_low[0:96] + f_high[0:96]
    for part in others:
        total = total + part[...]
    lane = lane_of(40)
    two = []
    for quarter in range(4):
        tile = exact_left(py2, total[24 * quarter : 24 * quarter + 24])
        wide = exact_right(tile, px2)
        for g in range(4):
            if 4 * quarter + g > 12:
                continue
            part = wide[:, 128 * (g // 2) : 128 * (g // 2) + 128]
            part = jnp.where(lane // 64 == g % 2, part, 0.0)
            two.append(part + pltpu.roll(part, 64, 1))
    one = []
    for p in range(11):
        even = two[p + 1]
        if p < 10:
            odd = 0.5625 * (two[p + 1] + two[p + 2]) - 0.0625 * (two[p] + two[p + 3])
        else:
            odd = jnp.zeros_like(even)
        value = jnp.where(lane < 64, even, odd) * mask2[z, p : p + 1, :]
        value = value + near2[40 * p : 40 * p + 40]
        if p < 5:
            value = value + f_low[96 + 40 * p : 136 + 40 * p]
        else:
            value = value + f_high[96 + 40 * (p - 5) : 136 + 40 * (p - 5)]
        tile = exact_left(py1, value)
        wide = exact_right(tile, px1)
        one.append(wide[:, 0:128])
        one.append(wide[:, 128:256])
    for f in range(35):
        if f % 2:
            value = one[(f + 3) // 2]
        else:
            h = f // 2
            value = 0.5625 * (one[h + 1] + one[h + 2]) - 0.0625 * (one[h] + one[h + 3])
        value = value * mask1[z, f] + near1[f]
        if f < 9:
            value = value + n_low[f]
        elif f > 24:
            value = value + n_high[f - 25]
        middle[f] = value
    doubled = jnp.concatenate([px0, px0], axis=0)
    for f in range(35):
        wide = jnp.concatenate(split(middle[f]), axis=1)
        out[f] = exact_left(py0, dot(wide, doubled))


def rise(tables, top, near2, f_low, f_high, others, near1, n_low, n_high):
    specs = [VMEM] * 5 + [SMEM] + [VMEM] * 2 + [VMEM] * 12
    return call(
        rise_body,
        [(35, 128, 128)],
        cost=400 << 20,
        in_specs=specs,
        out_specs=[VMEM],
        scratch_shapes=[pltpu.VMEM((35, 72, 128), F32)],
    )(*tables, top, near2, f_low, f_high, *others, near1, n_low, n_high)[0]


def along_z(taps, count, first, last, load):
    planes = {}

    def get(i):
        if not 0 <= i < count:
            return None
        if i not in planes:
            planes[i] = load(i)
        return planes[i]

    for k in range(first, last + 1):
        total = None
        for d in range(9):
            below, above = get(k - d), (get(k + d) if d else None)
            pair = below if above is None else above if below is None else below + above
            if pair is None:
                continue
            pair = pair * taps[d]
            total = pair if total is None else total + pair
        yield k, total


def near_z_body(taps, g, after, own, low, high):
    has_low, has_high = neighbours("gz")
    weights = [taps[0, d] for d in range(9)]
    for chunk in range(g.shape[1] // 8):
        rows = pl.ds(8 * chunk, 8)
        for k, total in along_z(weights, 64, -8, 71, lambda i: g[i, rows, :]):
            if k < 0:
                low[k + 8, rows, :] = total * has_low
            elif k < 64:
                own[k, rows, :] = total
            else:
                high[k - 64, rows, :] = total * has_high


def near_z(taps, g, after):
    block = lambda n: pl.BlockSpec((n, 16, 128), lambda i: (0, i, 0))
    return call(
        near_z_body,
        [(64, 128, 128), (8, 128, 128), (8, 128, 128)],
        cost=40 << 20,
        grid=(8,),
        in_specs=[SMEM, block(64), ANY],
        out_specs=[block(64), block(8), block(8)],
    )(taps, g, after)


def taps_at(taps, level, dist):
    value = jnp.zeros(dist.shape, F32)
    for d in range(9):
        value = jnp.where(dist == d, taps[level, d], value)
    return value


def near_table(taps, first, rows):
    r, c = grid_of(rows, 128)
    return taps_at(taps, 0, jnp.abs(r + first - c))


def near_y_body(taps, g, from_high, from_low, own, low, high, wide_table, low_table):
    step = pl.program_id(0)
    has_low, has_high = neighbours("gy")

    @pl.when(step == 0)
    def _():
        value = jnp.concatenate(
            [
                near_table(taps, 0, 128),
                near_table(taps, -8, 8) * has_low,
                near_table(taps, 128, 8) * has_high,
            ],
            axis=0,
        )
        upper, lower = split(value)
        wide_table[...] = jnp.concatenate([upper, upper], axis=1)
        low_table[...] = lower

    def work(values):
        for pair in range(4):
            both = jnp.concatenate([values[2 * pair], values[2 * pair + 1]], axis=1)
            upper, lower = split(both)
            full = dot(wide_table[...], jnp.concatenate([upper, lower], axis=0))
            full = full + dot(low_table[...], upper)
            for k in range(2):
                part = full[:, 128 * k : 128 * k + 128]
                at = 2 * pair + k
                own[at] = part[0:128]
                low[at] = part[128:136]
                high[at] = part[136:144]

    @pl.when(step == 0)
    def _():
        work([g[k] + from_low[k] for k in range(8)])

    @pl.when((step > 0) & (step < 7))
    def _():
        work([g[k] for k in range(8)])

    @pl.when(step == 7)
    def _():
        work([g[k] + from_high[k] for k in range(8)])


def near_y(taps, g, from_high, from_low):
    block = lambda n: pl.BlockSpec((8, n, 128), lambda i: (i, 0, 0))
    return call(
        near_y_body,
        [(64, 128, 128), (64, 8, 128), (64, 8, 128)],
        cost=2 << 30,
        grid=(8,),
        in_specs=[SMEM, block(128), VMEM, VMEM],
        out_specs=[block(128), block(8), block(8)],
        scratch_shapes=[pltpu.VMEM((144, 256), BF16), pltpu.VMEM((144, 128), BF16)],
    )(taps, g, from_high, from_low)


def near_x_body(taps, g, from_high, from_low, own, low, high, table, edge):
    has_low, has_high = neighbours("gx")

    @pl.when(pl.program_id(0) == 0)
    def _():
        upper, lower = split(near_table(taps, 0, 128))
        top = jnp.concatenate([upper, lower], axis=1)
        bottom = jnp.concatenate([upper, jnp.zeros_like(lower)], axis=1)
        table[...] = jnp.concatenate([top, bottom], axis=0)
        value = jnp.concatenate(
            [near_table(taps, -8, 8) * has_low, near_table(taps, 128, 8) * has_high], axis=0
        )
        upper, lower = split(value)
        edge[...] = jnp.concatenate([upper, upper, lower], axis=1)

    for k in range(8):
        value = jnp.concatenate(
            [g[k, 0:8] + from_low[k], g[k, 8:120], g[k, 120:128] + from_high[k]], axis=0
        )
        upper, lower = split(value)
        wide = jnp.concatenate([upper, lower], axis=1)
        full = dot(wide, table[...])
        own[k] = full[:, 0:128] + full[:, 128:256]
        sides = dot(edge[...], jnp.concatenate([wide, upper], axis=1), NT)
        low[k] = sides[0:8]
        high[k] = sides[8:16]


def near_x(taps, g, from_high, from_low):
    block = lambda n: pl.BlockSpec((8, n, 128), lambda i: (i, 0, 0))
    return call(
        near_x_body,
        [(64, 128, 128), (64, 8, 128), (64, 8, 128)],
        cost=2 << 30,
        grid=(8,),
        in_specs=[SMEM, block(128), block(8), block(8)],
        out_specs=[block(128), block(8), block(8)],
        scratch_shapes=[pltpu.VMEM((256, 256), BF16), pltpu.VMEM((16, 384), BF16)],
    )(taps, g, from_high, from_low)


def finest_body(near, from_high, from_low, coarse, out):
    at = 4 * pl.program_id(0)
    rows = []
    for k in range(8):
        rows.extend([from_high[k], from_low[k]])
    turned = jnp.concatenate(rows, axis=0).T
    lane = lane_of(128)
    edge = (lane < 8) | (lane >= 120)
    for k in range(8):
        h = k // 2
        if k % 2:
            value = 0.5625 * (coarse[at + h + 1] + coarse[at + h + 2]) - 0.0625 * (
                coarse[at + h] + coarse[at + h + 3]
            )
        else:
            value = coarse[at + h + 1]
        sides = pltpu.roll(turned, (128 - 16 * k - 8) % 128, 1)
        out[k] = value + near[k] + jnp.where(edge, sides, 0.0)


def finest(near, from_high, from_low, coarse):
    block = lambda n: pl.BlockSpec((8, n, 128), lambda i: (i, 0, 0))
    return call(
        finest_body,
        [(64, 128, 128)],
        cost=10 << 20,
        grid=(8,),
        in_specs=[block(128), block(8), block(8), VMEM],
        out_specs=[block(128)],
    )(near, from_high, from_low, coarse)[0]


def one_y_body(table, own1, from_high, from_low, ext, low, high):
    fh, fl = from_high[:, :2048], from_low[:, :2048]
    value = jnp.concatenate([own1[0:8] + fl, own1[8:56], own1[56:64] + fh], axis=0)
    full = mm(table[...], value)
    ext[...] = full[0:72]
    low[...] = full[72:88]
    high[...] = full[88:104]


def one_y(table, own1, from_high, from_low):
    return call(
        one_y_body,
        [(72, 2048), (16, 2048), (16, 2048)],
        cost=100 << 20,
        in_specs=[VMEM] * 4,
        out_specs=[VMEM] * 3,
    )(table, own1, from_high, from_low)


def one_x_body(table, edges, ext, from_high, from_low, out, low, high):
    tiles = []
    for t in range(16):
        lanes = slice(128 * t, 128 * t + 128)
        tiles.append(
            jnp.concatenate(
                [ext[0:16, lanes] + from_low[:, lanes], ext[16:56, lanes], ext[56:72, lanes] + from_high[:, lanes]],
                axis=0,
            )
        )
    for t in range(16):
        full = mm(tiles[t], table[...])
        out[2 * t] = full[:, 0:128]
        out[2 * t + 1] = full[:, 128:256]
    for q in range(4):
        full = mm(jnp.concatenate(tiles[4 * q : 4 * q + 4], axis=1), edges[...])
        low[72 * q : 72 * q + 72] = full[:, 0:128]
        high[72 * q : 72 * q + 72] = full[:, 128:256]


def one_x(table, edges, ext, from_high, from_low):
    return call(
        one_x_body,
        [(32, 72, 128), (288, 128), (288, 128)],
        cost=300 << 20,
        in_specs=[VMEM] * 5,
        out_specs=[VMEM] * 3,
    )(table, edges, ext, from_high, from_low)


def one_z_body(taps, ext, from_high, from_low, out, low, high):
    has_low, has_high = neighbours("gz")
    weights = [taps[1, d] * 0.5 for d in range(9)]
    group = lane_of(8) // 16

    @pl.loop(0, 9)
    def _(chunk):
        rows = pl.ds(pl.multiple_of(8 * chunk, 8), 8)

        def load(z):
            q, g = z // 8, z % 8
            at = pl.ds(pl.multiple_of(72 * q + 8 * chunk, 8), 8)
            a = jnp.where(group == g, from_low[at, :], 0.0)
            b = jnp.where(group == g, from_high[at, :], 0.0)
            if g:
                a = pltpu.roll(a, 128 - 16 * g, 1)
            b = pltpu.roll(b, (57 - 16 * g) % 128, 1)
            return ext[z, rows, :] + (a + b)

        for k, total in along_z(weights, 32, -8, 39, load):
            if k < 2:
                low[k + 8, rows, :] = total * has_low
            if k > 30:
                high[k - 31, rows, :] = total * has_high
            if -1 <= k < 34:
                out[k + 1, rows, :] = total * (has_low if k < 0 else has_high if k > 31 else 1.0)


def one_z(taps, ext, from_high, from_low):
    return call(
        one_z_body,
        [(35, 72, 128), (10, 72, 128), (9, 72, 128)],
        cost=20 << 20,
        in_specs=[SMEM] + [VMEM] * 3,
        out_specs=[VMEM] * 3,
    )(taps, ext, from_high, from_low)


def phi_at(dist):
    dist = jnp.abs(dist)
    return jnp.where(
        dist == 0, 1.0, jnp.where(dist == 1, 0.5625, jnp.where(dist == 3, -0.0625, 0.0))
    ).astype(F32)


def toeplitz(line, rows, offset):
    line = pltpu.roll(jnp.broadcast_to(line, (8, 128)), lax.rem(192 - offset, 128), 1)
    wide = jnp.broadcast_to(line[0:1], (rows, 128))
    return pltpu.roll(wide, 0, 1, stride=1, stride_axis=0)


def tables_body(taps, line, after, ytab, ttab, ntab, tcoef, ncoef, oney, onex, edges):
    z, y, x = [lax.axis_index(name) for name in AXES]

    def inside(r, place, own, total):
        where = r + place * own
        return (where >= 0) & (where < total)

    def near(level, dist, keep):
        return jnp.where(keep, taps_at(taps, level, jnp.abs(dist)), 0.0)

    j, c = grid_of(128, 128)
    right = jnp.where((j < 64) & (c < 32), phi_at(y * 32 + c - 2 * j), 0.0).astype(BF16)
    for s in range(4):
        first = lax.rem(y + s, 4) * 16 - 2
        left = toeplitz(line[...], 24, -first)
        i, l = grid_of(24, 128)
        keep = (l < 64) & (i < 21) & (first + i >= 0) & (first + i < 64)
        full = exact_right(jnp.where(keep, left, 0.0), right)
        ytab[24 * s : 24 * s + 24, :] = full[:, 0:32]
    i, c = grid_of(72, 32)
    keep = (i < 37) & inside(i - 2, y, 32, 128)
    keep = keep | ((i >= 42) & (i < 53) & (y > 0)) | ((i >= 56) & (i < 66) & (y < 3))
    r = jnp.where(i < 40, i - 2, jnp.where(i < 56, i - 50, i - 26))
    ytab[96:168, :] = near(2, r - c, keep)

    i, l = grid_of(128, 64)
    left = phi_at(x * 32 + i % 32 - 2 * l).astype(BF16)
    i, l = grid_of(64, 128)
    a, b = grid_of(128, 128)
    for s in range(4):
        first = lax.rem(x + s, 4) * 16 - 2
        right = toeplitz(line[...], 64, first)
        keep = (l < 21) & (first + l >= 0) & (first + l < 64)
        right = jnp.where(keep, right, 0.0)
        right = right + pltpu.roll(right, 32, 1)
        right = right + pltpu.roll(right, 64, 1)
        full = exact_left(left, right)
        ttab[:, 128 * s : 128 * s + 128] = jnp.where(a // 32 == b // 32, full, 0.0)
    i, l = grid_of(128, 256)
    r = l % 64 - 2
    keep = (l // 64 == i // 32) & (l % 64 < 37) & inside(r, x, 32, 128)
    ntab[:, 0:256] = near(2, r - i % 32, keep)
    i, l = grid_of(128, 128)
    same = l // 32 == i // 32
    ntab[:, 256:384] = near(2, l % 32 - 8 - i % 32, same & (l % 32 < 11) & (x > 0))
    ntab[:, 384:512] = near(2, l % 32 + 30 - i % 32, same & (l % 32 < 10) & (x < 3))

    i, l = grid_of(16, 64)
    left = phi_at(z * 16 + i - 2 * l).astype(BF16)
    i, l = grid_of(64, 128)
    parts = []
    for s in range(8):
        first = lax.rem(z + s, 8) * 8 - 2
        right = toeplitz(line[...], 64, first)
        keep = (l < 13) & (first + l >= 0) & (first + l < 64)
        parts.append(exact_left(left, jnp.where(keep, right, 0.0)))
    whole = jnp.concatenate(parts, axis=0) * 0.125
    i, l = grid_of(128, 128)
    for quarter in range(4):
        spread = jnp.where(i == 4 * quarter + l // 32, 1.0, 0.0).astype(BF16)
        full = exact_right(whole, spread)
        for s in range(8):
            at = (s * 4 + quarter) * 16
            tcoef[at : at + 16, :] = full[16 * s : 16 * s + 16]
    i, l = grid_of(16, 128)
    g = l // 64
    for p in range(22):
        if p < 11:
            r = g + (2 * p - 2)
            keep = (r <= 18) & inside(r, z, 16, 128)
        elif p < 17:
            r = g + (2 * (p - 11) - 8)
            keep = (r <= 2) & (z > 0)
        else:
            r = g + (2 * (p - 17) + 14)
            keep = (r <= 23) & (z < 7)
        ncoef[16 * p : 16 * p + 16, :] = near(2, r - i, keep) * 0.25

    i, c = grid_of(104, 64)
    keep = (i < 67) & inside(i - 1, y, 64, 256)
    keep = keep | ((i >= 73) & (i < 83) & (y > 0)) | ((i >= 88) & (i < 97) & (y < 3))
    r = jnp.where(i < 72, i - 1, jnp.where(i < 88, i - 81, i - 25))
    oney[...] = near(1, r - c, keep)
    i, l = grid_of(128, 256)
    r = l % 128 - 1
    keep = (l // 128 == i // 64) & (l % 128 < 67) & inside(r, x, 64, 256)
    onex[...] = near(1, r - i % 64, keep)
    i, l = grid_of(512, 128)
    same = l // 16 == i // 64
    edges[:, 0:128] = near(1, l % 16 - 8 - i % 64, same & (l % 16 < 10) & (x > 0))
    edges[:, 128:256] = near(1, l % 16 + 63 - i % 64, same & (l % 16 < 9) & (x < 3))


def tables(taps, top_taps, after):
    zero = jnp.zeros((1,), F32)
    line = jnp.concatenate([zero, top_taps[:0:-1], top_taps]).reshape(1, 128)
    return call(
        tables_body,
        [
            (168, 32), (128, 512), (128, 512), (512, 128),
            (352, 128), (104, 64), (128, 256), (512, 256),
        ],
        cost=50 << 20,
        in_specs=[SMEM, VMEM, ANY],
        out_specs=[VMEM] * 8,
    )(taps, line, after)


def rise_tables():
    def kron(table, groups):
        return np.stack([np.kron(np.eye(groups), t.T) for t in table])

    y2 = prolong_table(128, 4, 2, 3, 2, 3, (40, 24))
    x2 = kron(prolong_table(128, 4, 2, 3, 2, 3, (64, 32)), 4)
    y1 = prolong_table(256, 4, 1, 2, 2, 3, (72, 40))
    x1 = kron(prolong_table(256, 4, 1, 2, 2, 3, (128, 64)), 2)
    y0 = prolong_table(512, 4, 0, 0, 1, 2, (128, 72))
    x0 = kron(prolong_table(512, 4, 0, 0, 1, 2, (128, 128)), 1)
    mask2 = np.zeros((8, 11, 128), np.float32)
    mask1 = np.zeros((8, 35), np.float32)
    for place in range(8):
        for e in range(22):
            inside = 0 <= place * 16 - 2 + e < 128
            mask2[place, e // 2, 64 * (e % 2) : 64 * (e % 2) + 64] = inside
        for f in range(35):
            mask1[place, f] = 0 <= place * 32 - 1 + f < 256
    half = lambda table: jnp.asarray(table.astype(jnp.bfloat16))
    return half(y2), half(x2), jnp.asarray(mask2), half(y1), half(x1), jnp.asarray(mask1), half(y0), half(x0)


def per_device(charges, taps, top_taps):
    z, y, x = AXES
    chain = jnp.asarray(chain_tables(512, 4))

    one, two, low, high = coarse_z(charges)
    f_high, f_low = shift(low, z, -1), shift(high, z, 1)
    near, nlow, nhigh = near_z(taps, charges, two)
    ytab, ttab, ntab, tcoef, ncoef, oney, onex, edges = tables(taps, top_taps, two)
    nf_high, nf_low = shift(nlow, z, -1), shift(nhigh, z, 1)
    one, two, low, high = coarse_x(chain, one, two, f_high, f_low)
    f_high, f_low = shift(low, x, -1), shift(high, x, 1)
    one, two, low, high = coarse_y(chain, one, two, f_high, f_low)
    f_high, f_low = shift(low, y, -1), shift(high, y, 1)

    top, near2, up, down, far = top_y(ytab, two, f_high, f_low)
    g_low, g_high, g_far = shift(up, y, 1), shift(down, y, -1), shift(far, y, 2)
    near1, low, high = one_y(oney, one, f_high, f_low)
    h_high, h_low = shift(low, y, -1), shift(high, y, 1)

    near, nlow, nhigh = near_y(taps, near, nf_high, nf_low)
    nf_high, nf_low = shift(nlow, y, -1), shift(nhigh, y, 1)

    top, near2, up, down, far = top_x(ttab, ntab, top, near2, g_low, g_high, g_far)
    g_low, g_high, g_far = shift(up, x, 1), shift(down, x, -1), shift(far, x, 2)
    near1, low, high = one_x(onex, edges, near1, h_high, h_low)
    h_high, h_low = shift(low, x, -1), shift(high, x, 1)

    near, nlow, nhigh = near_x(taps, near, nf_high, nf_low)
    nf_high, nf_low = shift(nlow, x, -1), shift(nhigh, x, 1)

    top, near2, up, down, *others = top_z(tcoef, ncoef, top, near2, g_low, g_high, g_far)
    g_low, g_high = shift(up, z, 1), shift(down, z, -1)
    others = [shift(part, z, 2 + k) for k, part in enumerate(others)]
    near1, low, high = one_z(taps, near1, h_high, h_low)
    h_high, h_low = shift(low, z, -1), shift(high, z, 1)

    coarse = rise(rise_tables(), top, near2, g_low, g_high, others, near1, h_low, h_high)
    return finest(near, nf_high, nf_low, coarse)


def solution(mesh):
    return jax.shard_map(
        per_device,
        mesh=mesh,
        in_specs=(P("gz", "gy", "gx"), P(), P()),
        out_specs=P("gz", "gy", "gx"),
        check_vma=False,
    )
```

```python
import jax
import jax.numpy as jnp
import numpy as np
from jax import lax
from jax.experimental import pallas as pl
from jax.experimental.pallas import tpu as pltpu
from jax.sharding import PartitionSpec as P

AXES = ("gz", "gy", "gx")
F32 = jnp.float32
BF16 = jnp.bfloat16
NN = (((1,), (0,)), ((), ()))
NT = (((1,), (1,)), ((), ()))
ANY = pl.BlockSpec(memory_space=pl.ANY)
SMEM = pl.BlockSpec(memory_space=pltpu.SMEM)
VMEM = pl.BlockSpec(memory_space=pltpu.VMEM)


def phi(dist):
    dist = np.abs(dist)
    return np.where(
        dist == 0, 1.0, np.where(dist == 1, 0.5625, np.where(dist == 3, -0.0625, 0.0))
    )


def restrict_whole(size):
    rows = np.arange(size // 2)[:, None]
    cols = np.arange(size)[None, :]
    return phi(cols - 2 * rows)


def rows_of(whole, first, count):
    picked = np.zeros((count, whole.shape[1]))
    for r in range(count):
        if 0 <= first + r < whole.shape[0]:
            picked[r] = whole[first + r]
    return picked


def chain_tables(size, count):
    own0 = size // count
    first = restrict_whole(size)
    second = restrict_whole(size // 2) @ first
    stack = []
    for place in range(count):
        parts = []
        for whole, own, low, high in ((first, own0 // 2, 1, 2), (second, own0 // 4, 2, 3)):
            cols = whole[:, place * own0 : (place + 1) * own0]
            at = place * own
            parts.append(rows_of(cols, at, own))
            to_low = [np.zeros((4 - low, own0)), rows_of(cols, at - low, low)]
            to_high = [rows_of(cols, at + own, high), np.zeros((4 - high, own0))]
            parts.extend(to_low * 2 + to_high * 2)
        stack.append(np.concatenate(parts))
    return np.stack(stack).astype(jnp.bfloat16)


def prolong_table(total, count, low, high, from_low, from_high, shape):
    own = total // count
    stack = []
    for place in range(count):
        i = np.arange(-low, own + high)[:, None]
        coarse = np.arange(-from_low, own // 2 + from_high)[None, :]
        where = i + place * own
        table = phi(i - 2 * coarse) * ((where >= 0) & (where < total))
        whole = np.zeros(shape)
        whole[: table.shape[0], : table.shape[1]] = table
        stack.append(whole)
    return np.stack(stack)


def shift(value, name, step):
    count = lax.axis_size(name)
    return lax.ppermute(value, name, [(i, (i + step) % count) for i in range(count)])


def split(x):
    high = x.astype(BF16)
    return high, (x - high.astype(F32)).astype(BF16)


def dot(a, b, dims=NN):
    return lax.dot_general(a, b, dims, preferred_element_type=F32)


def mm(a, b):
    a_high, a_low = split(a)
    b_high, b_low = split(b)
    return dot(a_high, b_high) + (dot(a_low, b_high) + dot(a_high, b_low))


def exact_left(table, x):
    high, low = split(x)
    return dot(table, high) + dot(table, low)


def exact_right(x, table):
    high, low = split(x)
    return dot(high, table) + dot(low, table)


def neighbours(name):
    place = lax.axis_index(name)
    count = lax.axis_size(name)
    return (place > 0).astype(F32), (place < count - 1).astype(F32)


def call(body, outs, us, in_specs, out_specs, after=(), carry=(), vmem=8, **kwargs):
    count, kept = len(in_specs), len(outs)
    total = count + len(after) + len(carry)
    shapes = [jax.ShapeDtypeStruct(s, F32) for s in outs]
    shapes += [jax.ShapeDtypeStruct(a.shape, a.dtype) for a in carry]

    def run(*refs):
        inner = refs[total:]
        body(*refs[:count], *inner[:kept], *inner[kept + len(carry) :])

    kernel = pl.pallas_call(
        run,
        out_shape=shapes,
        in_specs=[*in_specs, *[ANY] * (total - count)],
        out_specs=[*out_specs, *[ANY] * len(carry)],
        input_output_aliases={count + len(after) + k: kept + k for k in range(len(carry))},
        compiler_params=pltpu.CompilerParams(vmem_limit_bytes=vmem * 1024 * 1024),
        cost_estimate=pl.CostEstimate(
            flops=1 << 10, bytes_accessed=int(us * 3.6e6), transcendentals=0
        ),
        **kwargs,
    )
    return lambda *args: kernel(*args, *after, *carry)


def grid_of(rows, cols):
    shape = (rows, cols)
    return lax.broadcasted_iota(jnp.int32, shape, 0), lax.broadcasted_iota(jnp.int32, shape, 1)


def lane_of(rows):
    return grid_of(rows, 128)[1]


def pack(first, second):
    return jnp.where(grid_of(8, 128)[0] < 4, first, second)


def unpack_low(tile, part):
    tile = tile if part else pltpu.roll(tile, 4, 0)
    return jnp.where(grid_of(8, 128)[0] >= 4, tile, 0.0)


def unpack_high(tile, part):
    tile = pltpu.roll(tile, 4, 0) if part else tile
    return jnp.where(grid_of(8, 128)[0] < 4, tile, 0.0)


def along_z(taps, count, first, last, load):
    planes = {}

    def get(i):
        if not 0 <= i < count:
            return None
        if i not in planes:
            planes[i] = load(i)
        return planes[i]

    for k in range(first, last + 1):
        total = None
        for d in range(9):
            below, above = get(k - d), (get(k + d) if d else None)
            pair = below if above is None else above if below is None else below + above
            if pair is None:
                continue
            pair = pair * taps[d]
            total = pair if total is None else total + pair
        yield k, total


def coarse_z_body(g, own1, own2, low, high):
    has_low, has_high = neighbours("gz")

    @pl.loop(0, 16)
    def _(chunk):
        rows = pl.ds(pl.multiple_of(8 * chunk, 8), 8)

        def weigh(at, count, get, low_at=0):
            total = None
            for offsets, weight in (((0,), 1.0), ((-1, 1), 0.5625), ((-3, 3), -0.0625)):
                part = None
                for o in offsets:
                    if low_at <= 2 * at + o < count:
                        value = get(2 * at + o)
                        part = value if part is None else part + value
                if part is not None:
                    part = part if weight == 1.0 else part * weight
                    total = part if total is None else total + part
            return total

        planes = {}

        def get(i):
            if i not in planes:
                planes[i] = g[i, rows, :]
            return planes[i]

        first = {}
        for j in range(-1, 34):
            first[j] = weigh(j, 64, get)
            if 0 <= j < 32:
                own1[j, rows, :] = first[j]
        for j, has in ((-1, has_low), (32, has_high), (33, has_high)):
            first[j] = first[j] * has
        low[0, rows, :] = first[-1]
        high[0, rows, :] = first[32]
        high[1, rows, :] = first[33]
        for k in range(-2, 19):
            value = weigh(k, 34, lambda j: first[j], -1)
            if k < 0:
                low[3 + k, rows, :] = value * has_low
            elif k < 16:
                own2[k, rows, :] = value
            else:
                high[k - 14, rows, :] = value * has_high


def coarse_z(g):
    return call(
        coarse_z_body,
        [(32, 128, 128), (16, 128, 128), (3, 128, 128), (5, 128, 128)],
        us=1.5,
        vmem=16,
        in_specs=[VMEM],
        out_specs=[VMEM] * 4,
    )(g)


def coarse_x_body(table, own1, own2, from_high, from_low, out1, out2, low, high):
    own_table = table[lax.axis_index("gx")]
    doubled = jnp.concatenate([own_table, own_table], axis=1)

    def work(source, out, at, pair, first, rows, extra=(None, None)):
        values = [source[2 * pair + k] for k in range(2)]
        values = [v if e is None else v + e for v, e in zip(values, extra)]
        wide = jnp.concatenate(split(jnp.concatenate(values, axis=0)), axis=1)
        full = dot(doubled[first : first + rows + 16], wide, NT)
        left, right = full[:, 0:128], full[:, 128:256]
        out[2 * pair] = left[:rows]
        out[2 * pair + 1] = right[:rows]
        low[at + pair] = pack(left[rows : rows + 8], right[rows : rows + 8])
        high[at + pair] = pack(left[rows + 8 :], right[rows + 8 :])

    for pair in range(16):
        extra = [from_low[0], from_low[1]] if pair == 0 else [None, None]
        if pair == 15:
            extra = [None, from_high[0]]
        work(own1, out1, 0, pair, 0, 64, extra)
    for pair in range(8):
        extra = [from_low[2], from_low[3]] if pair == 0 else [None, None]
        if pair == 1:
            extra = [from_low[4], None]
        if pair == 7:
            extra = [from_high[1], from_high[2]]
        work(own2, out2, 16, pair, 80, 32, extra)


def coarse_x(table, own1, own2, from_high, from_low, carry):
    return call(
        coarse_x_body,
        [(32, 64, 128), (16, 32, 128), (24, 8, 128), (24, 8, 128)],
        us=2,
        vmem=16,
        in_specs=[VMEM] * 5,
        out_specs=[VMEM] * 4,
        carry=carry,
    )(table, own1, own2, from_high, from_low)


def coarse_y_body(table, own1, own2, from_high, from_low, out1, out2, low, high):
    own_table = table[lax.axis_index("gy")]
    doubled = jnp.concatenate([own_table, own_table], axis=1)
    for source, base, first, rows, each, out, at in (
        (own1, 0, 0, 64, 4, out1, 0),
        (own2, 32, 80, 32, 8, out2, 1024),
    ):
        for group in range(source.shape[0] // each):
            parts = []
            for k in range(each):
                z = group * each + k
                pair, part = (base + z) // 2, (base + z) % 2
                parts.append(source[z, 0:8] + unpack_high(from_low[pair], part))
                parts.append(source[z, 8 : rows - 8])
                parts.append(source[z, rows - 8 : rows] + unpack_low(from_high[pair], part))
            wide = jnp.concatenate(split(jnp.concatenate(parts, axis=0)), axis=1)
            full = dot(doubled[first : first + rows + 16], wide, NT)
            lanes = pl.ds(256 * group, 256)
            out[:, lanes] = full[:rows]
            left, right = full[rows:, 0:128], full[rows:, 128:256]
            lanes = pl.ds(at + 128 * group, 128)
            low[:, lanes] = pack(left[0:8], right[0:8])
            high[:, lanes] = pack(left[8:16], right[8:16])


def coarse_y(table, own1, own2, from_high, from_low, after):
    return call(
        coarse_y_body,
        [(64, 2048), (32, 512), (8, 1280), (8, 1280)],
        us=0.6,
        in_specs=[VMEM] * 5,
        out_specs=[VMEM] * 4,
        after=after,
    )(table, own1, own2, from_high, from_low)


def spread(packed, unpack):
    tiles = []
    for t in range(packed.shape[1] // 128):
        tile = packed[:, 128 * t : 128 * t + 128]
        tiles.extend([unpack(tile, 0), unpack(tile, 1)])
    return jnp.concatenate(tiles, axis=1)


def with_edges(own, from_low, from_high):
    count = own.shape[0]
    parts = [own[0:8] + from_low, own[8 : count - 8], own[count - 8 :] + from_high]
    return jnp.concatenate(parts, axis=0)


def top_y_body(table, table1, own1, own2, from_high, from_low, top, near, near1, up, down, far):
    fl, fh = spread(from_low[...], unpack_high), spread(from_high[...], unpack_low)
    full = mm(table[...], with_edges(own2[...], fl[:, 2048:], fh[:, 2048:]))
    top[...] = full[0:24]
    up[0:24] = full[24:48]
    far[...] = full[48:72]
    down[0:24] = full[72:96]
    near[...] = full[96:136]
    down[24:40] = full[136:152]
    up[24:40] = full[152:168]
    full = mm(table1[...], with_edges(own1[...], fl[:, :2048], fh[:, :2048]))
    near1[...] = full[0:72]
    for t in range(4):
        lanes = slice(512 * t, 512 * t + 512)
        rows = slice(40 + 16 * t, 56 + 16 * t)
        down[rows] = full[72:88, lanes]
        up[rows] = full[88:104, lanes]


def top_y(table, table1, own1, own2, from_high, from_low, carry):
    return call(
        top_y_body,
        [(24, 512), (40, 512), (72, 2048), (104, 512), (104, 512), (24, 512)],
        us=1,
        in_specs=[VMEM] * 6,
        out_specs=[VMEM] * 6,
        carry=carry,
    )(table, table1, own1, own2, from_high, from_low)


def top_x_body(
    ttable, ntable, table1, edges, top, near, near1, f_low, f_high, f_far,
    otop, onear, onear1, up, down, far,
):
    total = top[...] + f_low[0:24] + (f_high[0:24] + f_far[...])
    extended = jnp.concatenate(
        [near[0:16] + f_low[24:40], near[16:24], near[24:40] + f_high[24:40]], axis=0
    )
    stacked = jnp.concatenate([total[:, 128 * t : 128 * t + 128] for t in range(4)], axis=0)
    full = mm(stacked, ttable[...])
    otop[...] = full[:, 0:128]
    up[0:96] = full[:, 128:256]
    far[...] = full[:, 256:384]
    down[0:96] = full[:, 384:512]
    stacked = jnp.concatenate([extended[:, 128 * t : 128 * t + 128] for t in range(4)], axis=0)
    full = mm(stacked, ntable[...])
    onear[...] = full[:, 0:256]
    down[96:256] = full[:, 256:384]
    up[96:256] = full[:, 384:512]
    tiles = []
    for t in range(16):
        lanes = slice(128 * t, 128 * t + 128)
        rows = slice(40 + 16 * (t // 4), 56 + 16 * (t // 4))
        part = slice(128 * (t % 4), 128 * (t % 4) + 128)
        parts = [near1[0:16, lanes] + f_low[rows, part], near1[16:56, lanes]]
        parts.append(near1[56:72, lanes] + f_high[rows, part])
        tiles.append(jnp.concatenate(parts, axis=0))
    for q in range(4):
        full = mm(jnp.concatenate(tiles[4 * q : 4 * q + 4], axis=1), edges[...])
        down[256 + 72 * q : 328 + 72 * q] = full[:, 0:128]
        up[256 + 72 * q : 328 + 72 * q] = full[:, 128:256]
    for t in range(16):
        full = mm(tiles[t], table1[...])
        onear1[2 * t] = full[:, 0:128]
        onear1[2 * t + 1] = full[:, 128:256]


def top_x(ttable, ntable, table1, edges, top, near, near1, f_low, f_high, f_far, after):
    return call(
        top_x_body,
        [(96, 128), (160, 256), (32, 72, 128), (544, 128), (544, 128), (96, 128)],
        us=2,
        in_specs=[VMEM] * 10,
        out_specs=[VMEM] * 6,
        after=after,
    )(ttable, ntable, table1, edges, top, near, near1, f_low, f_high, f_far)


def one_z(taps, ext, from_high, from_low, out, up, down):
    has_low, has_high = neighbours("gz")
    weights = [taps[1, d] * 0.5 for d in range(9)]
    group = lane_of(8) // 16

    @pl.loop(0, 9)
    def _(chunk):
        rows = pl.ds(pl.multiple_of(8 * chunk, 8), 8)

        def load(z):
            q, g = z // 8, z % 8
            at = pl.ds(pl.multiple_of(256 + 72 * q + 8 * chunk, 8), 8)
            a = jnp.where(group == g, from_low[at, :], 0.0)
            b = jnp.where(group == g, from_high[at, :], 0.0)
            if g:
                a = pltpu.roll(a, 128 - 16 * g, 1)
            b = pltpu.roll(b, (57 - 16 * g) % 128, 1)
            return ext[z, rows, :] + (a + b)

        for k, total in along_z(weights, 32, -8, 39, load):
            if k < 2:
                at = pl.ds(pl.multiple_of(72 * (k + 8) + 8 * chunk, 8), 8)
                down[at, :] = total * has_low
            if k > 30:
                at = pl.ds(pl.multiple_of(72 * (k - 31) + 8 * chunk, 8), 8)
                up[at, :] = total * has_high
            if -1 <= k < 34:
                out[k + 1, rows, :] = total * (has_low if k < 0 else has_high if k > 31 else 1.0)


def top_z_body(
    taps, tcoef, ncoef, top, near, ext, f_low, f_high, f_far, parts, partner, onear, out1, up, down
):
    total = top[...] + f_low[0:96] + (f_high[0:96] + f_far[...])
    group = lane_of(24) // 32
    planes = []
    for z in range(16):
        tile = total[24 * (z // 4) : 24 * (z // 4) + 24]
        part = jnp.where(group == z % 4, tile, 0.0)
        part = part + pltpu.roll(part, 32, 1)
        planes.append(part + pltpu.roll(part, 64, 1))
    for step in range(8):
        out = partner if step // 4 else parts
        for quarter in range(4):
            value = None
            for z in range(16):
                at = (step * 4 + quarter) * 16 + z
                part = planes[z] * tcoef[at : at + 1, :]
                value = part if value is None else value + part
            rows = 96 * (step % 4) + 24 * quarter
            out[rows : rows + 24] = value
    lane = lane_of(40)
    planes = []
    for z in range(16):
        tile, q = z // 4, z % 4
        rows = slice(40 * tile, 40 * tile + 40)
        part = near[rows, 128 * (q // 2) : 128 * (q // 2) + 128]
        part = jnp.where(lane // 64 == q % 2, part, 0.0)
        low = jnp.where(lane // 32 == q, f_low[96 + 40 * tile : 136 + 40 * tile], 0.0)
        high = jnp.where(lane // 32 == q, f_high[96 + 40 * tile : 136 + 40 * tile], 0.0)
        if q % 2:
            part = pltpu.roll(part, 64, 1)
        if q:
            low = pltpu.roll(low, 128 - 32 * q, 1)
        high = pltpu.roll(high, (26 - 32 * q) % 128, 1)
        part = part + (low + high)
        planes.append(part + pltpu.roll(part, 64, 1))
    for out, base, count, first, offset in (
        (onear, 0, 11, -2, 0),
        (down, 11, 6, -8, 720),
        (up, 17, 5, 14, 648),
    ):
        for p in range(count):
            value = None
            for z in range(16):
                r = first + 2 * p
                if min(abs(r - z), abs(r + 1 - z)) > 8:
                    continue
                at = (base + p) * 16 + z
                part = planes[z] * ncoef[at : at + 1, :]
                value = part if value is None else value + part
            out[offset + 40 * p : offset + 40 * p + 40] = value

    one_z(taps, ext, f_high, f_low, out1, up, down)


def top_z(taps, tcoef, ncoef, top, near, ext, f_low, f_high, f_far, carry):
    return call(
        top_z_body,
        [(384, 128), (384, 128), (440, 128), (35, 72, 128), (848, 128), (960, 128)],
        us=4,
        in_specs=[SMEM] + [VMEM] * 8,
        out_specs=[VMEM] * 6,
        carry=carry,
    )(taps, tcoef, ncoef, top, near, ext, f_low, f_high, f_far)


def top_sum_body(own, other, *outs):
    for k, out in enumerate(outs):
        rows = slice(96 * k, 96 * k + 96)
        out[...] = own[rows] + other[rows]


def top_sum(own, other):
    return call(
        top_sum_body, [(96, 128)] * 4, us=0.3, in_specs=[VMEM] * 2, out_specs=[VMEM] * 4
    )(own, other)


def rise_body(
    py2, px2, mask2, py1, px1, mask1, py0, px0, top, p1, p2, p3, near2, f_low, f_high,
    near1, out, middle,
):
    z, y, x = [lax.axis_index(name) for name in AXES]
    py2, py1, py0 = py2[y], py1[y], py0[y]
    px2, px1, px0 = px2[x], px1[x], px0[x]
    total = (top[...] + p1[...]) + (p2[...] + p3[...])
    lane = lane_of(40)
    two = []
    for quarter in range(4):
        tile = exact_left(py2, total[24 * quarter : 24 * quarter + 24])
        wide = exact_right(tile, px2)
        for g in range(4):
            if 4 * quarter + g > 12:
                continue
            part = wide[:, 128 * (g // 2) : 128 * (g // 2) + 128]
            part = jnp.where(lane // 64 == g % 2, part, 0.0)
            two.append(part + pltpu.roll(part, 64, 1))
    one = []
    for p in range(11):
        even = two[p + 1]
        if p < 10:
            odd = 0.5625 * (two[p + 1] + two[p + 2]) - 0.0625 * (two[p] + two[p + 3])
        else:
            odd = jnp.zeros_like(even)
        value = jnp.where(lane < 64, even, odd) * mask2[z, p : p + 1, :]
        value = value + near2[40 * p : 40 * p + 40]
        if p < 5:
            value = value + f_low[648 + 40 * p : 688 + 40 * p]
        else:
            value = value + f_high[720 + 40 * (p - 5) : 760 + 40 * (p - 5)]
        tile = exact_left(py1, value)
        wide = exact_right(tile, px1)
        one.append(wide[:, 0:128])
        one.append(wide[:, 128:256])
    for f in range(35):
        if f % 2:
            value = one[(f + 3) // 2]
        else:
            h = f // 2
            value = 0.5625 * (one[h + 1] + one[h + 2]) - 0.0625 * (one[h] + one[h + 3])
        value = value * mask1[z, f] + near1[f]
        if f < 9:
            value = value + f_low[72 * f : 72 * f + 72]
        elif f > 24:
            value = value + f_high[72 * (f - 25) : 72 * (f - 24)]
        middle[f] = value
    doubled = jnp.concatenate([px0, px0], axis=0)
    for f in range(35):
        wide = jnp.concatenate(split(middle[f]), axis=1)
        out[f] = exact_left(py0, dot(wide, doubled))


def rise(tables, top, others, near2, f_low, f_high, near1):
    return call(
        rise_body,
        [(35, 128, 128)],
        us=5,
        in_specs=[VMEM] * 5 + [SMEM] + [VMEM] * 10,
        out_specs=[VMEM],
        scratch_shapes=[pltpu.VMEM((35, 72, 128), F32)],
    )(*tables, top, *others, near2, f_low, f_high, near1)[0]


def near_z_body(taps, g, own, low, high):
    has_low, has_high = neighbours("gz")
    weights = [taps[0, d] for d in range(9)]

    @pl.loop(0, 16)
    def _(chunk):
        rows = pl.ds(pl.multiple_of(8 * chunk, 8), 8)
        for k, total in along_z(weights, 64, -8, 71, lambda i: g[i, rows, :]):
            if k < 0:
                low[k + 8, rows, :] = total * has_low
            elif k < 64:
                own[k, rows, :] = total
            else:
                high[k - 64, rows, :] = total * has_high


def near_z(taps, g, after):
    return call(
        near_z_body,
        [(64, 128, 128), (8, 128, 128), (8, 128, 128)],
        us=6,
        vmem=16,
        in_specs=[SMEM, VMEM],
        out_specs=[VMEM] * 3,
        after=after,
    )(taps, g)


def taps_at(taps, level, dist):
    value = jnp.zeros(dist.shape, F32)
    for d in range(9):
        value = jnp.where(dist == d, taps[level, d], value)
    return value


def near_at(taps, dist):
    return taps_at(taps, 0, jnp.abs(dist))


def near_x_body(taps, g, from_high, from_low, own, low, high):
    has_low, has_high = neighbours("gx")
    row, col = grid_of(128, 128)
    edge = near_at(taps, row - col + 8) * jnp.where(col < 8, has_low, 0.0)
    edge = edge + near_at(taps, row - col - 120) * jnp.where((col >= 8) & (col < 16), has_high, 0.0)
    upper, lower = split(jnp.concatenate([near_at(taps, row - col), edge], axis=1))
    table = jnp.concatenate([upper, upper], axis=0)

    def work(k, q, j, extra=None):
        value = g[k] if extra is None else g[k] + extra
        first, second = split(value)
        full = dot(jnp.concatenate([first, second], axis=1), table) + dot(first, lower)
        own[k] = full[:, 0:128]
        low[q, :, 8 * j : 8 * j + 8] = full[:, 128:136]
        high[q, :, 8 * j : 8 * j + 8] = full[:, 136:144]

    for j in range(16):
        work(j, 0, j, from_low[j] if j < 8 else None)

    @pl.loop(1, 3)
    def _(q):
        for j in range(16):
            work(16 * q + j, q, j)

    for j in range(16):
        work(48 + j, 3, j, from_high[j - 8] if j >= 8 else None)


def near_x(taps, g, from_high, from_low, after):
    return call(
        near_x_body,
        [(64, 128, 128), (4, 128, 128), (4, 128, 128)],
        us=5,
        vmem=16,
        in_specs=[SMEM] + [VMEM] * 3,
        out_specs=[VMEM] * 3,
        after=after,
    )(taps, g, from_high, from_low)


def near_y_body(taps, g, from_high, from_low, own, low, high):
    has_low, has_high = neighbours("gy")
    row, col = grid_of(8, 128)
    value = jnp.concatenate(
        [
            near_at(taps, grid_of(128, 128)[0] - grid_of(128, 128)[1]),
            near_at(taps, row - col - 8) * has_low,
            near_at(taps, row - col + 128) * has_high,
        ],
        axis=0,
    )
    upper, lower = split(value)
    wide_table = jnp.concatenate([upper, upper], axis=1)
    lane = lane_of(128)

    def load(q, j):
        left = pltpu.roll(from_low[q], (128 - 8 * j) % 128, 1)
        right = pltpu.roll(from_high[q], (120 - 8 * j) % 128, 1)
        sides = jnp.where(lane < 8, left, jnp.where(lane >= 120, right, 0.0))
        return g[16 * q + j] + sides

    @pl.loop(0, 4)
    def _(q):
        for pair in range(8):
            values = [load(q, 2 * pair + k) for k in range(2)]
            first, second = split(jnp.concatenate(values, axis=1))
            full = dot(wide_table, jnp.concatenate([first, second], axis=0))
            full = full + dot(lower, first)
            for k in range(2):
                at = 16 * q + 2 * pair + k
                part = full[:, 128 * k : 128 * k + 128]
                own[at] = part[0:128]
                low[at] = part[128:136]
                high[at] = part[136:144]


def near_y(taps, g, from_high, from_low, after):
    return call(
        near_y_body,
        [(64, 128, 128), (64, 8, 128), (64, 8, 128)],
        us=4,
        vmem=16,
        in_specs=[SMEM] + [VMEM] * 3,
        out_specs=[VMEM] * 3,
        after=after,
    )(taps, g, from_high, from_low)


def finest_body(near, from_high, from_low, coarse, out):
    step = pl.program_id(0)
    at = 4 * step
    planes = [coarse[at + h] for h in range(7)]
    for k in range(8):
        h = k // 2
        value = planes[h + 1]
        if k % 2:
            value = 0.5625 * (value + planes[h + 2]) - 0.0625 * (planes[h] + planes[h + 3])
        value = value + near[8 * step + k]
        out[k, 0:8] = value[0:8] + from_low[8 * step + k]
        out[k, 8:120] = value[8:120]
        out[k, 120:128] = value[120:128] + from_high[8 * step + k]


def finest(near, from_high, from_low, coarse):
    return call(
        finest_body,
        [(64, 128, 128)],
        us=4,
        vmem=16,
        grid=(8,),
        in_specs=[VMEM] * 4,
        out_specs=[pl.BlockSpec((8, 128, 128), lambda i: (i, 0, 0))],
    )(near, from_high, from_low, coarse)[0]


def phi_at(dist):
    dist = jnp.abs(dist)
    return jnp.where(
        dist == 0, 1.0, jnp.where(dist == 1, 0.5625, jnp.where(dist == 3, -0.0625, 0.0))
    ).astype(F32)


def toeplitz(line, rows, offset):
    line = pltpu.roll(line, lax.rem(192 - offset, 128), 1)
    wide = jnp.broadcast_to(line[0:1], (rows, 128))
    return pltpu.roll(wide, 0, 1, stride=1, stride_axis=0)


def tables_body(taps, top_taps, ytab, ttab, ntab, tcoef, ncoef, oney, onex, edges):
    z, y, x = [lax.axis_index(name) for name in AXES]
    dist = jnp.abs(lane_of(8) - 64)
    line = jnp.zeros((8, 128), F32)
    for d in range(64):
        line = jnp.where(dist == d, top_taps[d], line)

    def inside(r, place, own, total):
        where = r + place * own
        return (where >= 0) & (where < total)

    def near(level, dist, keep):
        return jnp.where(keep, taps_at(taps, level, jnp.abs(dist)), 0.0)

    j, c = grid_of(128, 128)
    right = jnp.where((j < 64) & (c < 32), phi_at(y * 32 + c - 2 * j), 0.0).astype(BF16)
    for s in range(4):
        first = lax.rem(y + s, 4) * 16 - 2
        left = toeplitz(line, 24, -first)
        i, l = grid_of(24, 128)
        keep = (l < 64) & (i < 21) & (first + i >= 0) & (first + i < 64)
        full = exact_right(jnp.where(keep, left, 0.0), right)
        ytab[24 * s : 24 * s + 24, :] = full[:, 0:32]
    i, c = grid_of(72, 32)
    keep = (i < 37) & inside(i - 2, y, 32, 128)
    keep = keep | ((i >= 42) & (i < 53) & (y > 0)) | ((i >= 56) & (i < 66) & (y < 3))
    r = jnp.where(i < 40, i - 2, jnp.where(i < 56, i - 50, i - 26))
    ytab[96:168, :] = near(2, r - c, keep)

    i, l = grid_of(128, 64)
    left = phi_at(x * 32 + i % 32 - 2 * l).astype(BF16)
    i, l = grid_of(64, 128)
    a, b = grid_of(128, 128)
    for s in range(4):
        first = lax.rem(x + s, 4) * 16 - 2
        right = toeplitz(line, 64, first)
        keep = (l < 21) & (first + l >= 0) & (first + l < 64)
        right = jnp.where(keep, right, 0.0)
        right = right + pltpu.roll(right, 32, 1)
        right = right + pltpu.roll(right, 64, 1)
        full = exact_left(left, right)
        ttab[:, 128 * s : 128 * s + 128] = jnp.where(a // 32 == b // 32, full, 0.0)
    i, l = grid_of(128, 256)
    r = l % 64 - 2
    keep = (l // 64 == i // 32) & (l % 64 < 37) & inside(r, x, 32, 128)
    ntab[:, 0:256] = near(2, r - i % 32, keep)
    i, l = grid_of(128, 128)
    same = l // 32 == i // 32
    ntab[:, 256:384] = near(2, l % 32 - 8 - i % 32, same & (l % 32 < 11) & (x > 0))
    ntab[:, 384:512] = near(2, l % 32 + 30 - i % 32, same & (l % 32 < 10) & (x < 3))

    i, l = grid_of(16, 64)
    left = phi_at(z * 16 + i - 2 * l).astype(BF16)
    i, l = grid_of(64, 128)
    parts = []
    for s in range(8):
        chip, core = lax.rem(z // 2 + s % 4, 4), lax.rem(z + s // 4, 2)
        first = (2 * chip + core) * 8 - 2
        right = toeplitz(line, 64, first)
        keep = (l < 13) & (first + l >= 0) & (first + l < 64)
        parts.append(exact_left(left, jnp.where(keep, right, 0.0)))
    whole = jnp.concatenate(parts, axis=0) * 0.125
    i, l = grid_of(128, 128)
    for quarter in range(4):
        spread = jnp.where(i == 4 * quarter + l // 32, 1.0, 0.0).astype(BF16)
        full = exact_right(whole, spread)
        for s in range(8):
            at = (s * 4 + quarter) * 16
            tcoef[at : at + 16, :] = full[16 * s : 16 * s + 16]
    i, l = grid_of(16, 128)
    g = l // 64
    for p in range(22):
        if p < 11:
            r = g + (2 * p - 2)
            keep = (r <= 18) & inside(r, z, 16, 128)
        elif p < 17:
            r = g + (2 * (p - 11) - 8)
            keep = (r <= 2) & (z > 0)
        else:
            r = g + (2 * (p - 17) + 14)
            keep = (r <= 23) & (z < 7)
        ncoef[16 * p : 16 * p + 16, :] = near(2, r - i, keep) * 0.25

    i, c = grid_of(104, 64)
    keep = (i < 67) & inside(i - 1, y, 64, 256)
    keep = keep | ((i >= 73) & (i < 83) & (y > 0)) | ((i >= 88) & (i < 97) & (y < 3))
    r = jnp.where(i < 72, i - 1, jnp.where(i < 88, i - 81, i - 25))
    oney[...] = near(1, r - c, keep)
    i, l = grid_of(128, 256)
    r = l % 128 - 1
    keep = (l // 128 == i // 64) & (l % 128 < 67) & inside(r, x, 64, 256)
    onex[...] = near(1, r - i % 64, keep)
    i, l = grid_of(512, 128)
    same = l // 16 == i // 64
    edges[:, 0:128] = near(1, l % 16 - 8 - i % 64, same & (l % 16 < 10) & (x > 0))
    edges[:, 128:256] = near(1, l % 16 + 63 - i % 64, same & (l % 16 < 9) & (x < 3))


def tables(taps, top_taps, after):
    return call(
        tables_body,
        [
            (168, 32), (128, 512), (128, 512), (512, 128),
            (352, 128), (104, 64), (128, 256), (512, 256),
        ],
        us=2,
        in_specs=[SMEM, SMEM],
        out_specs=[VMEM] * 8,
        after=after,
    )(taps, top_taps)


def rise_tables():
    def kron(table, groups):
        return np.stack([np.kron(np.eye(groups), t.T) for t in table])

    y2 = prolong_table(128, 4, 2, 3, 2, 3, (40, 24))
    x2 = kron(prolong_table(128, 4, 2, 3, 2, 3, (64, 32)), 4)
    y1 = prolong_table(256, 4, 1, 2, 2, 3, (72, 40))
    x1 = kron(prolong_table(256, 4, 1, 2, 2, 3, (128, 64)), 2)
    y0 = prolong_table(512, 4, 0, 0, 1, 2, (128, 72))
    x0 = kron(prolong_table(512, 4, 0, 0, 1, 2, (128, 128)), 1)
    mask2 = np.zeros((8, 11, 128), np.float32)
    mask1 = np.zeros((8, 35), np.float32)
    for place in range(8):
        for e in range(22):
            inside = 0 <= place * 16 - 2 + e < 128
            mask2[place, e // 2, 64 * (e % 2) : 64 * (e % 2) + 64] = inside
        for f in range(35):
            mask1[place, f] = 0 <= place * 32 - 1 + f < 256
    half = lambda table: jnp.asarray(table.astype(jnp.bfloat16))
    return half(y2), half(x2), jnp.asarray(mask2), half(y1), half(x1), jnp.asarray(mask1), half(y0), half(x0)


def per_device(charges, taps, top_taps):
    z, y, x = AXES
    chain = jnp.asarray(chain_tables(512, 4))

    one, two, low, high = coarse_z(charges)
    f_high, f_low = shift(low, z, -1), shift(high, z, 1)
    near, *nsides = near_z(taps, charges, (two,))

    one, two, low, high, *nsides = coarse_x(chain, one, two, f_high, f_low, nsides)
    f_high, f_low = shift(low, x, -1), shift(high, x, 1)
    nf_high, nf_low = shift(nsides[0], z, -1), shift(nsides[1], z, 1)
    ytab, ttab, ntab, tcoef, ncoef, oney, onex, edges = tables(taps, top_taps, (two,))

    one, two, low, high = coarse_y(chain, one, two, f_high, f_low, (ytab,))
    f_high, f_low = shift(low, y, -1), shift(high, y, 1)
    near, *nsides = near_x(taps, near, nf_high, nf_low, (two,))

    top, near2, near1, up, down, far, *nsides = top_y(ytab, oney, one, two, f_high, f_low, nsides)
    f_low, f_high, f_far = shift(up, y, 1), shift(down, y, -1), shift(far, y, 2)
    nf_high, nf_low = shift(nsides[0], x, -1), shift(nsides[1], x, 1)

    top, near2, near1, up, down, far = top_x(
        ttab, ntab, onex, edges, top, near2, near1, f_low, f_high, f_far, (nf_high, nf_low)
    )
    f_low, f_high, f_far = shift(up, x, 1), shift(down, x, -1), shift(far, x, 2)
    near, *nsides = near_y(taps, near, nf_high, nf_low, (top,))

    top, partner, near2, near1, up, down, *nsides = top_z(
        taps, tcoef, ncoef, top, near2, near1, f_low, f_high, f_far, nsides
    )
    count = lax.axis_size(z)
    partner = lax.ppermute(partner, z, [(i, i ^ 1) for i in range(count)])
    f_low, f_high = shift(up, z, 1), shift(down, z, -1)
    nf_high, nf_low = shift(nsides[0], y, -1), shift(nsides[1], y, 1)
    top, *others = top_sum(top, partner)
    others = [shift(part, z, 2 + 2 * k) for k, part in enumerate(others)]

    coarse = rise(rise_tables(), top, others, near2, f_low, f_high, near1)
    return finest(near, nf_high, nf_low, coarse)


def solution(mesh):
    return jax.shard_map(
        per_device,
        mesh=mesh,
        in_specs=(P("gz", "gy", "gx"), P(), P()),
        out_specs=P("gz", "gy", "gx"),
        check_vma=False,
    )
```

```python
import jax
import jax.numpy as jnp
import numpy as np
from jax import lax
from jax.experimental import pallas as pl
from jax.experimental.pallas import tpu as pltpu
from jax.sharding import PartitionSpec as P

AXES = ("gz", "gy", "gx")
F32 = jnp.float32
BF16 = jnp.bfloat16
NN = (((1,), (0,)), ((), ()))
NT = (((1,), (1,)), ((), ()))
ANY = pl.BlockSpec(memory_space=pl.ANY)
SMEM = pl.BlockSpec(memory_space=pltpu.SMEM)
VMEM = pl.BlockSpec(memory_space=pltpu.VMEM)


def phi(dist):
    dist = np.abs(dist)
    return np.where(
        dist == 0, 1.0, np.where(dist == 1, 0.5625, np.where(dist == 3, -0.0625, 0.0))
    )


def restrict_whole(size):
    rows = np.arange(size // 2)[:, None]
    cols = np.arange(size)[None, :]
    return phi(cols - 2 * rows)


def rows_of(whole, first, count):
    picked = np.zeros((count, whole.shape[1]))
    for r in range(count):
        if 0 <= first + r < whole.shape[0]:
            picked[r] = whole[first + r]
    return picked


def chain_tables(size, count):
    own0 = size // count
    first = restrict_whole(size)
    second = restrict_whole(size // 2) @ first
    stack = []
    for place in range(count):
        parts = []
        for whole, own, low, high in ((first, own0 // 2, 1, 2), (second, own0 // 4, 2, 3)):
            cols = whole[:, place * own0 : (place + 1) * own0]
            at = place * own
            parts.append(rows_of(cols, at, own))
            to_low = [np.zeros((4 - low, own0)), rows_of(cols, at - low, low)]
            to_high = [rows_of(cols, at + own, high), np.zeros((4 - high, own0))]
            parts.extend(to_low * 2 + to_high * 2)
        stack.append(np.concatenate(parts))
    return np.stack(stack).astype(jnp.bfloat16)


def chain_rows(size, count):
    own0 = size // count
    first = restrict_whole(size)
    second = restrict_whole(size // 2) @ first
    stacks = []
    for whole, own, low, high, rows in ((first, own0 // 2, 1, 2, 80), (second, own0 // 4, 2, 3, 48)):
        stack = np.zeros((count, rows, own0))
        for place in range(count):
            cols = whole[:, place * own0 : (place + 1) * own0]
            stack[place, : own + low + high] = rows_of(cols, place * own - low, own + low + high)
        stacks.append(stack.astype(jnp.bfloat16))
    return stacks


def prolong_table(total, count, low, high, from_low, from_high, shape):
    own = total // count
    stack = []
    for place in range(count):
        i = np.arange(-low, own + high)[:, None]
        coarse = np.arange(-from_low, own // 2 + from_high)[None, :]
        where = i + place * own
        table = phi(i - 2 * coarse) * ((where >= 0) & (where < total))
        whole = np.zeros(shape)
        whole[: table.shape[0], : table.shape[1]] = table
        stack.append(whole)
    return np.stack(stack)


def shift(value, name, step):
    count = lax.axis_size(name)
    return lax.ppermute(value, name, [(i, (i + step) % count) for i in range(count)])


def split(x):
    high = x.astype(BF16)
    return high, (x - high.astype(F32)).astype(BF16)


def dot(a, b, dims=NN):
    return lax.dot_general(a, b, dims, preferred_element_type=F32)


def mm(a, b):
    a_high, a_low = split(a)
    b_high, b_low = split(b)
    return dot(a_high, b_high) + (dot(a_low, b_high) + dot(a_high, b_low))


def exact_left(table, x):
    high, low = split(x)
    return dot(table, high) + dot(table, low)


def exact_right(x, table):
    high, low = split(x)
    return dot(high, table) + dot(low, table)


def neighbours(name):
    place = lax.axis_index(name)
    count = lax.axis_size(name)
    return (place > 0).astype(F32), (place < count - 1).astype(F32)


def call(body, outs, us, in_specs, out_specs, after=(), carry=(), vmem=8, **kwargs):
    count, kept = len(in_specs), len(outs)
    total = count + len(after) + len(carry)
    shapes = [jax.ShapeDtypeStruct(s, F32) for s in outs]
    shapes += [jax.ShapeDtypeStruct(a.shape, a.dtype) for a in carry]

    def run(*refs):
        inner = refs[total:]
        body(*refs[:count], *inner[:kept], *inner[kept + len(carry) :])

    kernel = pl.pallas_call(
        run,
        out_shape=shapes,
        in_specs=[*in_specs, *[ANY] * (total - count)],
        out_specs=[*out_specs, *[ANY] * len(carry)],
        input_output_aliases={count + len(after) + k: kept + k for k in range(len(carry))},
        compiler_params=pltpu.CompilerParams(vmem_limit_bytes=vmem * 1024 * 1024),
        cost_estimate=pl.CostEstimate(
            flops=int(us * 1.15e10), bytes_accessed=int(us * 3.6e8), transcendentals=0
        ),
        **kwargs,
    )
    return lambda *args: kernel(*args, *after, *carry)


def grid_of(rows, cols):
    shape = (rows, cols)
    return lax.broadcasted_iota(jnp.int32, shape, 0), lax.broadcasted_iota(jnp.int32, shape, 1)


def lane_of(rows):
    return grid_of(rows, 128)[1]


def pack(first, second):
    return jnp.where(grid_of(8, 128)[0] < 4, first, second)


def unpack_low(tile, part):
    tile = tile if part else pltpu.roll(tile, 4, 0)
    return jnp.where(grid_of(8, 128)[0] >= 4, tile, 0.0)


def unpack_high(tile, part):
    tile = pltpu.roll(tile, 4, 0) if part else tile
    return jnp.where(grid_of(8, 128)[0] < 4, tile, 0.0)


def along_z(taps, count, first, last, load):
    planes = {}

    def get(i):
        if not 0 <= i < count:
            return None
        if i not in planes:
            planes[i] = load(i)
        return planes[i]

    for k in range(first, last + 1):
        total = None
        for d in range(9):
            below, above = get(k - d), (get(k + d) if d else None)
            pair = below if above is None else above if below is None else below + above
            if pair is None:
                continue
            pair = pair * taps[d]
            total = pair if total is None else total + pair
        yield k, total


def coarse_z_body(g, own1, own2, low, high):
    has_low, has_high = neighbours("gz")

    @pl.loop(0, 16)
    def _(chunk):
        rows = pl.ds(pl.multiple_of(8 * chunk, 8), 8)

        def weigh(at, count, get, low_at=0):
            total = None
            for offsets, weight in (((0,), 1.0), ((-1, 1), 0.5625), ((-3, 3), -0.0625)):
                part = None
                for o in offsets:
                    if low_at <= 2 * at + o < count:
                        value = get(2 * at + o)
                        part = value if part is None else part + value
                if part is not None:
                    part = part if weight == 1.0 else part * weight
                    total = part if total is None else total + part
            return total

        planes = {}

        def get(i):
            if i not in planes:
                planes[i] = g[i, rows, :]
            return planes[i]

        first = {}
        for j in range(-1, 34):
            first[j] = weigh(j, 64, get)
            if 0 <= j < 32:
                own1[j, rows, :] = first[j]
        for j, has in ((-1, has_low), (32, has_high), (33, has_high)):
            first[j] = first[j] * has
        low[0, rows, :] = first[-1]
        high[0, rows, :] = first[32]
        high[1, rows, :] = first[33]
        for k in range(-2, 19):
            value = weigh(k, 34, lambda j: first[j], -1)
            if k < 0:
                low[3 + k, rows, :] = value * has_low
            elif k < 16:
                own2[k, rows, :] = value
            else:
                high[k - 14, rows, :] = value * has_high


def coarse_z(g):
    return call(
        coarse_z_body,
        [(32, 128, 128), (16, 128, 128), (3, 128, 128), (5, 128, 128)],
        us=1.5,
        vmem=16,
        in_specs=[VMEM],
        out_specs=[VMEM] * 4,
    )(g)


def coarse_x_body(table, own1, own2, from_high, from_low, out1, out2, low, high):
    own_table = table[lax.axis_index("gx")]
    doubled = jnp.concatenate([own_table, own_table], axis=1)

    def work(source, out, at, pair, first, rows, extra=(None, None)):
        values = [source[2 * pair + k] for k in range(2)]
        values = [v if e is None else v + e for v, e in zip(values, extra)]
        wide = jnp.concatenate(split(jnp.concatenate(values, axis=0)), axis=1)
        full = dot(doubled[first : first + rows + 16], wide, NT)
        left, right = full[:, 0:128], full[:, 128:256]
        out[2 * pair] = left[:rows]
        out[2 * pair + 1] = right[:rows]
        low[at + pair] = pack(left[rows : rows + 8], right[rows : rows + 8])
        high[at + pair] = pack(left[rows + 8 :], right[rows + 8 :])

    for pair in range(16):
        extra = [from_low[0], from_low[1]] if pair == 0 else [None, None]
        if pair == 15:
            extra = [None, from_high[0]]
        work(own1, out1, 0, pair, 0, 64, extra)
    for pair in range(8):
        extra = [from_low[2], from_low[3]] if pair == 0 else [None, None]
        if pair == 1:
            extra = [from_low[4], None]
        if pair == 7:
            extra = [from_high[1], from_high[2]]
        work(own2, out2, 16, pair, 80, 32, extra)


def coarse_x(table, own1, own2, from_high, from_low, carry):
    return call(
        coarse_x_body,
        [(32, 64, 128), (16, 32, 128), (24, 8, 128), (24, 8, 128)],
        us=2,
        vmem=16,
        in_specs=[VMEM] * 5,
        out_specs=[VMEM] * 4,
        carry=carry,
    )(table, own1, own2, from_high, from_low)


def stacked(own, from_low, from_high, first, planes):
    parts = []
    for k in range(planes):
        z = first + k
        at, part = divmod(z, 2)
        rows = own.shape[1]
        parts.append(own[z, 0:8] + unpack_high(from_low[at], part))
        parts.append(own[z, 8 : rows - 8])
        parts.append(own[z, rows - 8 : rows] + unpack_low(from_high[at], part))
    return jnp.concatenate(parts, axis=0)


def mm_turned(table, value):
    t_high, t_low = split(table)
    high, low = split(value)
    wide = jnp.concatenate([t_high, t_low, t_high], axis=1)
    return dot(wide, jnp.concatenate([high, high, low], axis=1), NT)


def top_y_body(table, table1, own1, own2, from_high, from_low, top, near, near1, up, down, far):
    half = from_low.at[16:24], from_high.at[16:24]
    full = mm_turned(table[...], stacked(own2, *half, 0, 16))
    top[...] = full[0:24]
    up[0:24] = full[24:48]
    far[...] = full[48:72]
    down[0:24] = full[72:96]
    near[...] = full[96:136]
    down[24:40] = full[136:152]
    up[24:40] = full[152:168]
    for q in range(8):
        full = mm_turned(table1[...], stacked(own1, from_low, from_high, 4 * q, 4))
        near1[:, 256 * q : 256 * q + 256] = full[0:72]
        lanes = slice(256 * (q % 2), 256 * (q % 2) + 256)
        rows = slice(40 + 16 * (q // 2), 56 + 16 * (q // 2))
        down[rows, lanes] = full[72:88]
        up[rows, lanes] = full[88:104]


def top_y(table, table1, own1, own2, from_high, from_low, carry):
    return call(
        top_y_body,
        [(24, 512), (40, 512), (72, 2048), (104, 512), (104, 512), (24, 512)],
        us=1.5,
        in_specs=[VMEM] * 6,
        out_specs=[VMEM] * 6,
        carry=carry,
    )(table, table1, own1, own2, from_high, from_low)


def top_x_body(
    ttable, ntable, table1, edges, top, near, near1, f_low, f_high, f_far,
    otop, onear, onear1, up, down, far,
):
    total = top[...] + f_low[0:24] + (f_high[0:24] + f_far[...])
    extended = jnp.concatenate(
        [near[0:16] + f_low[24:40], near[16:24], near[24:40] + f_high[24:40]], axis=0
    )
    stacked = jnp.concatenate([total[:, 128 * t : 128 * t + 128] for t in range(4)], axis=0)
    full = mm(stacked, ttable[...])
    otop[...] = full[:, 0:128]
    up[0:96] = full[:, 128:256]
    far[...] = full[:, 256:384]
    down[0:96] = full[:, 384:512]
    stacked = jnp.concatenate([extended[:, 128 * t : 128 * t + 128] for t in range(4)], axis=0)
    full = mm(stacked, ntable[...])
    onear[...] = full[:, 0:256]
    down[96:256] = full[:, 256:384]
    up[96:256] = full[:, 384:512]
    tiles = []
    for t in range(16):
        lanes = slice(128 * t, 128 * t + 128)
        rows = slice(40 + 16 * (t // 4), 56 + 16 * (t // 4))
        part = slice(128 * (t % 4), 128 * (t % 4) + 128)
        parts = [near1[0:16, lanes] + f_low[rows, part], near1[16:56, lanes]]
        parts.append(near1[56:72, lanes] + f_high[rows, part])
        tiles.append(jnp.concatenate(parts, axis=0))
    for q in range(4):
        full = mm(jnp.concatenate(tiles[4 * q : 4 * q + 4], axis=1), edges[...])
        down[256 + 72 * q : 328 + 72 * q] = full[:, 0:128]
        up[256 + 72 * q : 328 + 72 * q] = full[:, 128:256]
    for t in range(16):
        full = mm(tiles[t], table1[...])
        onear1[2 * t] = full[:, 0:128]
        onear1[2 * t + 1] = full[:, 128:256]


def top_x(ttable, ntable, table1, edges, top, near, near1, f_low, f_high, f_far, after):
    return call(
        top_x_body,
        [(96, 128), (160, 256), (32, 72, 128), (544, 128), (544, 128), (96, 128)],
        us=2,
        in_specs=[VMEM] * 10,
        out_specs=[VMEM] * 6,
        after=after,
    )(ttable, ntable, table1, edges, top, near, near1, f_low, f_high, f_far)


def folded(values):
    lane = lane_of(values[0].shape[0])
    tail = jnp.zeros_like(values[0])
    for k, value in enumerate(values):
        tail = jnp.where(lane // 4 == k, pltpu.roll(value, (64 + 4 * k) % 128, 1), tail)
    packed = []
    for k in range(0, len(values), 2):
        second = pltpu.roll(values[k + 1], 64, 1) if k + 1 < len(values) else jnp.zeros_like(tail)
        packed.append(jnp.where(lane < 64, values[k], second))
    return [*packed, tail]


def unfold(buffer, k, tail):
    first = buffer[72 * (k // 2) : 72 * (k // 2) + 72]
    lane = lane_of(72)
    first = pltpu.roll(first, 64, 1) if k % 2 else first
    last = pltpu.roll(buffer[72 * tail : 72 * tail + 72], (64 - 4 * k) % 128, 1)
    return jnp.where(lane < 64, first, jnp.where(lane < 68, last, 0.0))


def one_z(taps, ext, from_high, from_low, out, up, down):
    has_low, has_high = neighbours("gz")
    weights = [taps[1, d] * 0.5 for d in range(9)]
    group = lane_of(8) // 16

    @pl.loop(0, 9)
    def _(chunk):
        rows = pl.ds(pl.multiple_of(8 * chunk, 8), 8)

        def load(z):
            q, g = z // 8, z % 8
            at = pl.ds(pl.multiple_of(256 + 72 * q + 8 * chunk, 8), 8)
            a = jnp.where(group == g, from_low[at, :], 0.0)
            b = jnp.where(group == g, from_high[at, :], 0.0)
            if g:
                a = pltpu.roll(a, 128 - 16 * g, 1)
            b = pltpu.roll(b, (57 - 16 * g) % 128, 1)
            return ext[z, rows, :] + (a + b)

        lows, highs = [], []
        for k, total in along_z(weights, 32, -8, 39, load):
            if k < 2:
                lows.append(total * has_low)
            if k > 30:
                highs.append(total * has_high)
            if -1 <= k < 34:
                out[k + 1, rows, :] = total * (has_low if k < 0 else has_high if k > 31 else 1.0)
        for values, buffer in ((lows, down), (highs, up)):
            for k, value in enumerate(folded(values)):
                buffer[pl.ds(pl.multiple_of(72 * k + 8 * chunk, 8), 8), :] = value


def top_z_body(
    taps, tcoef, ncoef, top, near, ext, f_low, f_high, f_far, parts, partner, onear, out1, up, down
):
    total = top[...] + f_low[0:96] + (f_high[0:96] + f_far[...])
    group = lane_of(24) // 32
    planes = []
    for z in range(16):
        tile = total[24 * (z // 4) : 24 * (z // 4) + 24]
        part = jnp.where(group == z % 4, tile, 0.0)
        part = part + pltpu.roll(part, 32, 1)
        planes.append(part + pltpu.roll(part, 64, 1))
    for step in range(8):
        out = partner if step // 4 else parts
        for quarter in range(4):
            value = None
            for z in range(16):
                at = (step * 4 + quarter) * 16 + z
                part = planes[z] * tcoef[at : at + 1, :]
                value = part if value is None else value + part
            rows = 96 * (step % 4) + 24 * quarter
            out[rows : rows + 24] = value
    lane = lane_of(40)
    planes = []
    for z in range(16):
        tile, q = z // 4, z % 4
        rows = slice(40 * tile, 40 * tile + 40)
        part = near[rows, 128 * (q // 2) : 128 * (q // 2) + 128]
        part = jnp.where(lane // 64 == q % 2, part, 0.0)
        low = jnp.where(lane // 32 == q, f_low[96 + 40 * tile : 136 + 40 * tile], 0.0)
        high = jnp.where(lane // 32 == q, f_high[96 + 40 * tile : 136 + 40 * tile], 0.0)
        if q % 2:
            part = pltpu.roll(part, 64, 1)
        if q:
            low = pltpu.roll(low, 128 - 32 * q, 1)
        high = pltpu.roll(high, (26 - 32 * q) % 128, 1)
        part = part + (low + high)
        planes.append(part + pltpu.roll(part, 64, 1))
    for out, base, count, first, offset in (
        (onear, 0, 11, -2, 0),
        (down, 11, 6, -8, 432),
        (up, 17, 5, 14, 432),
    ):
        for p in range(count):
            value = None
            for z in range(16):
                r = first + 2 * p
                if min(abs(r - z), abs(r + 1 - z)) > 8:
                    continue
                at = (base + p) * 16 + z
                part = planes[z] * ncoef[at : at + 1, :]
                value = part if value is None else value + part
            out[offset + 40 * p : offset + 40 * p + 40] = value

    one_z(taps, ext, f_high, f_low, out1, up, down)


def top_z(taps, tcoef, ncoef, top, near, ext, f_low, f_high, f_far, after):
    return call(
        top_z_body,
        [(384, 128), (384, 128), (440, 128), (35, 72, 128), (632, 128), (672, 128)],
        us=4,
        in_specs=[SMEM] + [VMEM] * 8,
        out_specs=[VMEM] * 6,
        after=after,
    )(taps, tcoef, ncoef, top, near, ext, f_low, f_high, f_far)


def top_sum_body(own, other, *outs):
    for k, out in enumerate(outs):
        rows = slice(96 * k, 96 * k + 96)
        out[...] = own[rows] + other[rows]


def top_sum(own, other, after):
    return call(
        top_sum_body,
        [(96, 128)] * 4,
        us=0.3,
        in_specs=[VMEM] * 2,
        out_specs=[VMEM] * 4,
        after=after,
    )(own, other)


def rise_body(
    py2, px2, mask2, py1, px1, mask1, py0, px0, top, p1, p2, p3, near2, f_low, f_high,
    near1, out, middle,
):
    z, y, x = [lax.axis_index(name) for name in AXES]
    py2, py1, py0 = py2[y], py1[y], py0[y]
    px2, px1, px0 = px2[x], px1[x], px0[x]
    total = (top[...] + p1[...]) + (p2[...] + p3[...])
    lane = lane_of(40)
    wide = jnp.concatenate([total[24 * q : 24 * q + 24] for q in range(4)], axis=1)
    tile = exact_left(py2, wide)
    rows = jnp.concatenate([tile[:, 128 * q : 128 * q + 128] for q in range(4)], axis=0)
    rows = exact_right(rows, px2)
    two = []
    for k in range(13):
        q, g = divmod(k, 4)
        part = rows[40 * q : 40 * q + 40, 128 * (g // 2) : 128 * (g // 2) + 128]
        part = jnp.where(lane // 64 == g % 2, part, 0.0)
        two.append(part + pltpu.roll(part, 64, 1))
    values = []
    for p in range(11):
        even = two[p + 1]
        if p < 10:
            odd = 0.5625 * (two[p + 1] + two[p + 2]) - 0.0625 * (two[p] + two[p + 3])
        else:
            odd = jnp.zeros_like(even)
        value = jnp.where(lane < 64, even, odd) * mask2[z, p : p + 1, :]
        value = value + near2[40 * p : 40 * p + 40]
        if p < 5:
            value = value + f_low[432 + 40 * p : 472 + 40 * p]
        else:
            value = value + f_high[432 + 40 * (p - 5) : 472 + 40 * (p - 5)]
        values.append(value)
    tile = exact_left(py1, jnp.concatenate(values, axis=1))
    rows = jnp.concatenate([tile[:, 128 * p : 128 * p + 128] for p in range(11)], axis=0)
    rows = exact_right(rows, px1)
    one = []
    for p in range(11):
        one.append(rows[72 * p : 72 * p + 72, 0:128])
        one.append(rows[72 * p : 72 * p + 72, 128:256])
    for f in range(35):
        if f % 2:
            value = one[(f + 3) // 2]
        else:
            h = f // 2
            value = 0.5625 * (one[h + 1] + one[h + 2]) - 0.0625 * (one[h] + one[h + 3])
        value = value * mask1[z, f] + near1[f]
        if f < 9:
            value = value + unfold(f_low, f, 5)
        elif f > 24:
            value = value + unfold(f_high, f - 25, 5)
        middle[72 * f : 72 * f + 72] = value
    doubled = jnp.concatenate([px0, px0], axis=0)
    left = jnp.concatenate([py0, py0], axis=1)
    for group in range(5):
        part = middle[504 * group : 504 * group + 504]
        part = dot(jnp.concatenate(split(part), axis=1), doubled)
        wide = jnp.concatenate([part[72 * k : 72 * k + 72] for k in range(7)], axis=1)
        full = dot(left, jnp.concatenate(split(wide), axis=0))
        for k in range(7):
            out[7 * group + k] = full[:, 128 * k : 128 * k + 128]


def rise(tables, top, others, near2, f_low, f_high, near1):
    return call(
        rise_body,
        [(35, 128, 128)],
        us=5,
        in_specs=[VMEM] * 5 + [SMEM] + [VMEM] * 10,
        out_specs=[VMEM],
        scratch_shapes=[pltpu.VMEM((2520, 128), F32)],
    )(*tables, top, *others, near2, f_low, f_high, near1)[0]


def near_z_body(taps, g, own, low, high):
    has_low, has_high = neighbours("gz")
    weights = [taps[0, d] for d in range(9)]

    @pl.loop(0, 16)
    def _(chunk):
        rows = pl.ds(pl.multiple_of(8 * chunk, 8), 8)
        for k, total in along_z(weights, 64, -8, 71, lambda i: g[i, rows, :]):
            if k < 0:
                low[k + 8, rows, :] = total * has_low
            elif k < 64:
                own[k, rows, :] = total
            else:
                high[k - 64, rows, :] = total * has_high


def near_z(taps, g, after):
    return call(
        near_z_body,
        [(64, 128, 128), (8, 128, 128), (8, 128, 128)],
        us=6,
        vmem=16,
        in_specs=[SMEM, VMEM],
        out_specs=[VMEM] * 3,
        after=after,
    )(taps, g)


def taps_at(taps, level, dist):
    value = jnp.zeros(dist.shape, F32)
    for d in range(9):
        value = jnp.where(dist == d, taps[level, d], value)
    return value


def near_at(taps, dist):
    return taps_at(taps, 0, jnp.abs(dist))


def near_x_body(taps, g, from_high, from_low, own, low, high):
    has_low, has_high = neighbours("gx")
    row, col = grid_of(128, 128)
    edge = near_at(taps, row - col + 8) * jnp.where(col < 8, has_low, 0.0)
    edge = edge + near_at(taps, row - col - 120) * jnp.where((col >= 8) & (col < 16), has_high, 0.0)
    upper, lower = split(jnp.concatenate([near_at(taps, row - col), edge], axis=1))
    table = jnp.concatenate([upper, upper], axis=0)

    def work(k, q, j, extra=None):
        value = g[k] if extra is None else g[k] + extra
        first, second = split(value)
        full = dot(jnp.concatenate([first, second], axis=1), table) + dot(first, lower)
        own[k] = full[:, 0:128]
        low[q, :, 8 * j : 8 * j + 8] = full[:, 128:136]
        high[q, :, 8 * j : 8 * j + 8] = full[:, 136:144]

    for j in range(16):
        work(j, 0, j, from_low[j] if j < 8 else None)

    @pl.loop(1, 3)
    def _(q):
        for j in range(16):
            work(16 * q + j, q, j)

    for j in range(16):
        work(48 + j, 3, j, from_high[j - 8] if j >= 8 else None)


def near_x(taps, g, from_high, from_low, after):
    return call(
        near_x_body,
        [(64, 128, 128), (4, 128, 128), (4, 128, 128)],
        us=5,
        vmem=16,
        in_specs=[SMEM] + [VMEM] * 3,
        out_specs=[VMEM] * 3,
        after=after,
    )(taps, g, from_high, from_low)


def near_y_body(taps, g, from_high, from_low, own, low, high):
    has_low, has_high = neighbours("gy")
    row, col = grid_of(8, 128)
    value = jnp.concatenate(
        [
            near_at(taps, grid_of(128, 128)[0] - grid_of(128, 128)[1]),
            near_at(taps, row - col - 8) * has_low,
            near_at(taps, row - col + 128) * has_high,
        ],
        axis=0,
    )
    upper, lower = split(value)
    wide_table = jnp.concatenate([upper, upper], axis=1)
    lane = lane_of(128)

    def load(q, j):
        left = pltpu.roll(from_low[q], (128 - 8 * j) % 128, 1)
        right = pltpu.roll(from_high[q], (120 - 8 * j) % 128, 1)
        sides = jnp.where(lane < 8, left, jnp.where(lane >= 120, right, 0.0))
        return g[16 * q + j] + sides

    @pl.loop(0, 4)
    def _(q):
        for pair in range(8):
            values = [load(q, 2 * pair + k) for k in range(2)]
            first, second = split(jnp.concatenate(values, axis=1))
            full = dot(wide_table, jnp.concatenate([first, second], axis=0))
            full = full + dot(lower, first)
            for k in range(2):
                at = 16 * q + 2 * pair + k
                part = full[:, 128 * k : 128 * k + 128]
                own[at] = part[0:128]
                low[at] = part[128:136]
                high[at] = part[136:144]


def near_y(taps, g, from_high, from_low, after):
    return call(
        near_y_body,
        [(64, 128, 128), (64, 8, 128), (64, 8, 128)],
        us=4,
        vmem=16,
        in_specs=[SMEM] + [VMEM] * 3,
        out_specs=[VMEM] * 3,
        after=after,
    )(taps, g, from_high, from_low)


def finest_body(near, from_high, from_low, coarse, out):
    step = pl.program_id(0)
    at = 4 * step
    planes = [coarse[at + h] for h in range(7)]
    for k in range(8):
        h = k // 2
        value = planes[h + 1]
        if k % 2:
            value = 0.5625 * (value + planes[h + 2]) - 0.0625 * (planes[h] + planes[h + 3])
        value = value + near[8 * step + k]
        out[k, 0:8] = value[0:8] + from_low[8 * step + k]
        out[k, 8:120] = value[8:120]
        out[k, 120:128] = value[120:128] + from_high[8 * step + k]


def finest(near, from_high, from_low, coarse):
    return call(
        finest_body,
        [(64, 128, 128)],
        us=4,
        vmem=16,
        grid=(8,),
        in_specs=[VMEM] * 4,
        out_specs=[pl.BlockSpec((8, 128, 128), lambda i: (i, 0, 0))],
    )(near, from_high, from_low, coarse)[0]


def phi_at(dist):
    dist = jnp.abs(dist)
    return jnp.where(
        dist == 0, 1.0, jnp.where(dist == 1, 0.5625, jnp.where(dist == 3, -0.0625, 0.0))
    ).astype(F32)


def toeplitz(line, rows, offset):
    line = pltpu.roll(line, lax.rem(192 - offset, 128), 1)
    wide = jnp.broadcast_to(line[0:1], (rows, 128))
    return pltpu.roll(wide, 0, 1, stride=1, stride_axis=0)


def tables_body(taps, top_taps, rows1, rows2, ytab, ttab, ntab, tcoef, ncoef, oney, onex, edges):
    z, y, x = [lax.axis_index(name) for name in AXES]
    dist = jnp.abs(lane_of(8) - 64)
    line = jnp.zeros((8, 128), F32)
    for d in range(64):
        line = jnp.where(dist == d, top_taps[d], line)

    def inside(r, place, own, total):
        where = r + place * own
        return (where >= 0) & (where < total)

    def near(level, dist, keep):
        return jnp.where(keep, taps_at(taps, level, jnp.abs(dist)), 0.0)

    second = rows2[y]
    j, c = grid_of(128, 48)
    keep = (j < 64) & (c < 37) & inside(c - 2, y, 32, 128)
    right = jnp.where(keep, phi_at(y * 32 + c - 2 - 2 * j), 0.0).astype(BF16)
    for s in range(4):
        first = lax.rem(y + s, 4) * 16 - 2
        left = toeplitz(line, 24, -first)
        i, l = grid_of(24, 128)
        keep = (l < 64) & (i < 21) & (first + i >= 0) & (first + i < 64)
        full = exact_right(jnp.where(keep, left, 0.0), right)
        ytab[24 * s : 24 * s + 24, :] = exact_right(full, second)
    i, c = grid_of(72, 48)
    keep = (i < 37) & inside(i - 2, y, 32, 128)
    keep = keep | ((i >= 40) & (i < 53) & (y > 0)) | ((i >= 56) & (i < 69) & (y < 3))
    r = jnp.where(i < 40, i - 2, jnp.where(i < 56, i - 50, i - 26))
    ytab[96:168, :] = exact_right(near(2, r - (c - 2), keep), second)

    i, l = grid_of(128, 64)
    left = phi_at(x * 32 + i % 32 - 2 * l).astype(BF16)
    i, l = grid_of(64, 128)
    a, b = grid_of(128, 128)
    for s in range(4):
        first = lax.rem(x + s, 4) * 16 - 2
        right = toeplitz(line, 64, first)
        keep = (l < 21) & (first + l >= 0) & (first + l < 64)
        right = jnp.where(keep, right, 0.0)
        right = right + pltpu.roll(right, 32, 1)
        right = right + pltpu.roll(right, 64, 1)
        full = exact_left(left, right)
        ttab[:, 128 * s : 128 * s + 128] = jnp.where(a // 32 == b // 32, full, 0.0)
    i, l = grid_of(128, 256)
    r = l % 64 - 2
    keep = (l // 64 == i // 32) & (l % 64 < 37) & inside(r, x, 32, 128)
    ntab[:, 0:256] = near(2, r - i % 32, keep)
    i, l = grid_of(128, 128)
    same = l // 32 == i // 32
    ntab[:, 256:384] = near(2, l % 32 - 8 - i % 32, same & (l % 32 < 11) & (x > 0))
    ntab[:, 384:512] = near(2, l % 32 + 30 - i % 32, same & (l % 32 < 10) & (x < 3))

    i, l = grid_of(16, 64)
    left = phi_at(z * 16 + i - 2 * l).astype(BF16)
    i, l = grid_of(64, 128)
    parts = []
    for s in range(8):
        chip, core = lax.rem(z // 2 + s % 4, 4), lax.rem(z + s // 4, 2)
        first = (2 * chip + core) * 8 - 2
        right = toeplitz(line, 64, first)
        keep = (l < 13) & (first + l >= 0) & (first + l < 64)
        parts.append(exact_left(left, jnp.where(keep, right, 0.0)))
    whole = jnp.concatenate(parts, axis=0) * 0.125
    i, l = grid_of(128, 128)
    for quarter in range(4):
        spread = jnp.where(i == 4 * quarter + l // 32, 1.0, 0.0).astype(BF16)
        full = exact_right(whole, spread)
        for s in range(8):
            at = (s * 4 + quarter) * 16
            tcoef[at : at + 16, :] = full[16 * s : 16 * s + 16]
    i, l = grid_of(16, 128)
    g = l // 64
    for p in range(22):
        if p < 11:
            r = g + (2 * p - 2)
            keep = (r <= 18) & inside(r, z, 16, 128)
        elif p < 17:
            r = g + (2 * (p - 11) - 8)
            keep = (r <= 2) & (z > 0)
        else:
            r = g + (2 * (p - 17) + 14)
            keep = (r <= 23) & (z < 7)
        ncoef[16 * p : 16 * p + 16, :] = near(2, r - i, keep) * 0.25

    i, c = grid_of(104, 80)
    keep = (i < 67) & inside(i - 1, y, 64, 256)
    keep = keep | ((i >= 72) & (i < 83) & (y > 0)) | ((i >= 88) & (i < 99) & (y < 3))
    r = jnp.where(i < 72, i - 1, jnp.where(i < 88, i - 81, i - 25))
    oney[...] = exact_right(near(1, r - (c - 1), keep), rows1[y])
    i, l = grid_of(128, 256)
    r = l % 128 - 1
    keep = (l // 128 == i // 64) & (l % 128 < 67) & inside(r, x, 64, 256)
    onex[...] = near(1, r - i % 64, keep)
    i, l = grid_of(512, 128)
    same = l // 16 == i // 64
    edges[:, 0:128] = near(1, l % 16 - 8 - i % 64, same & (l % 16 < 10) & (x > 0))
    edges[:, 128:256] = near(1, l % 16 + 63 - i % 64, same & (l % 16 < 9) & (x < 3))


def tables(taps, top_taps, after):
    return call(
        tables_body,
        [
            (168, 128), (128, 512), (128, 512), (512, 128),
            (352, 128), (104, 128), (128, 256), (512, 256),
        ],
        us=2,
        in_specs=[SMEM, SMEM, VMEM, VMEM],
        out_specs=[VMEM] * 8,
        after=after,
    )(taps, top_taps, *[jnp.asarray(t) for t in chain_rows(512, 4)])


def rise_tables():
    def kron(table, groups):
        return np.stack([np.kron(np.eye(groups), t.T) for t in table])

    y2 = prolong_table(128, 4, 2, 3, 2, 3, (40, 24))
    x2 = kron(prolong_table(128, 4, 2, 3, 2, 3, (64, 32)), 4)
    y1 = prolong_table(256, 4, 1, 2, 2, 3, (72, 40))
    x1 = kron(prolong_table(256, 4, 1, 2, 2, 3, (128, 64)), 2)
    y0 = prolong_table(512, 4, 0, 0, 1, 2, (128, 72))
    x0 = kron(prolong_table(512, 4, 0, 0, 1, 2, (128, 128)), 1)
    mask2 = np.zeros((8, 11, 128), np.float32)
    mask1 = np.zeros((8, 35), np.float32)
    for place in range(8):
        for e in range(22):
            inside = 0 <= place * 16 - 2 + e < 128
            mask2[place, e // 2, 64 * (e % 2) : 64 * (e % 2) + 64] = inside
        for f in range(35):
            mask1[place, f] = 0 <= place * 32 - 1 + f < 256
    half = lambda table: jnp.asarray(table.astype(jnp.bfloat16))
    return half(y2), half(x2), jnp.asarray(mask2), half(y1), half(x1), jnp.asarray(mask1), half(y0), half(x0)


def per_device(charges, taps, top_taps):
    z, y, x = AXES
    chain = jnp.asarray(chain_tables(512, 4))

    one, two, low, high = coarse_z(charges)
    f_high, f_low = shift(low, z, -1), shift(high, z, 1)
    near, *nsides = near_z(taps, charges, (two,))
    nf_high, nf_low = shift(nsides[0], z, -1), shift(nsides[1], z, 1)
    ytab, ttab, ntab, tcoef, ncoef, oney, onex, edges = tables(taps, top_taps, (two,))

    one, two, low, high = coarse_x(chain, one, two, f_high, f_low, ())
    f_high, f_low = shift(low, x, -1), shift(high, x, 1)
    near, *nsides = near_x(taps, near, nf_high, nf_low, (two,))

    top, near2, near1, up, down, far, *nsides = top_y(ytab, oney, one, two, f_high, f_low, nsides)
    f_low, f_high, f_far = shift(up, y, 1), shift(down, y, -1), shift(far, y, 2)
    nf_high, nf_low = shift(nsides[0], x, -1), shift(nsides[1], x, 1)

    top, near2, near1, up, down, far = top_x(
        ttab, ntab, onex, edges, top, near2, near1, f_low, f_high, f_far, (nf_high, nf_low)
    )
    f_low, f_high, f_far = shift(up, x, 1), shift(down, x, -1), shift(far, x, 2)
    near, *nsides = near_y(taps, near, nf_high, nf_low, (top,))

    top, partner, near2, near1, up, down = top_z(
        taps, tcoef, ncoef, top, near2, near1, f_low, f_high, f_far, (nsides[0],)
    )
    count = lax.axis_size(z)
    partner = lax.ppermute(partner, z, [(i, i ^ 1) for i in range(count)])
    f_low, f_high = shift(up, z, 1), shift(down, z, -1)
    nf_high, nf_low = shift(nsides[0], y, -1), shift(nsides[1], y, 1)
    top, *others = top_sum(top, partner, (nf_high, nf_low))
    others = [shift(part, z, 2 + 2 * k) for k, part in enumerate(others)]

    coarse = rise(rise_tables(), top, others, near2, f_low, f_high, near1)
    return finest(near, nf_high, nf_low, coarse)


def solution(mesh):
    return jax.shard_map(
        per_device,
        mesh=mesh,
        in_specs=(P("gz", "gy", "gx"), P(), P()),
        out_specs=P("gz", "gy", "gx"),
        check_vma=False,
    )
```

```python
import jax
import jax.numpy as jnp
import numpy as np
from jax import lax
from jax.experimental import pallas as pl
from jax.experimental.pallas import tpu as pltpu
from jax.sharding import PartitionSpec as P

AXES = ("gz", "gy", "gx")
F32 = jnp.float32
BF16 = jnp.bfloat16
NN = (((1,), (0,)), ((), ()))
NT = (((1,), (1,)), ((), ()))
ANY = pl.BlockSpec(memory_space=pl.ANY)
SMEM = pl.BlockSpec(memory_space=pltpu.SMEM)
VMEM = pl.BlockSpec(memory_space=pltpu.VMEM)


def phi(dist):
    dist = np.abs(dist)
    return np.where(
        dist == 0, 1.0, np.where(dist == 1, 0.5625, np.where(dist == 3, -0.0625, 0.0))
    )


def restrict_whole(size):
    rows = np.arange(size // 2)[:, None]
    cols = np.arange(size)[None, :]
    return phi(cols - 2 * rows)


def rows_of(whole, first, count):
    picked = np.zeros((count, whole.shape[1]))
    for r in range(count):
        if 0 <= first + r < whole.shape[0]:
            picked[r] = whole[first + r]
    return picked


def chain_tables(size, count):
    own0 = size // count
    first = restrict_whole(size)
    second = restrict_whole(size // 2) @ first
    stack = []
    for place in range(count):
        parts = []
        for whole, own, low, high in ((first, own0 // 2, 1, 2), (second, own0 // 4, 2, 3)):
            cols = whole[:, place * own0 : (place + 1) * own0]
            at = place * own
            parts.append(rows_of(cols, at, own))
            to_low = [np.zeros((4 - low, own0)), rows_of(cols, at - low, low)]
            to_high = [rows_of(cols, at + own, high), np.zeros((4 - high, own0))]
            parts.extend(to_low * 2 + to_high * 2)
        stack.append(np.concatenate(parts))
    return np.stack(stack).astype(jnp.bfloat16)


def chain_rows(size, count):
    own0 = size // count
    first = restrict_whole(size)
    second = restrict_whole(size // 2) @ first
    stacks = []
    for whole, own, low, high, rows in ((first, own0 // 2, 1, 2, 80), (second, own0 // 4, 2, 3, 48)):
        stack = np.zeros((count, rows, own0))
        for place in range(count):
            cols = whole[:, place * own0 : (place + 1) * own0]
            stack[place, : own + low + high] = rows_of(cols, place * own - low, own + low + high)
        stacks.append(stack.astype(jnp.bfloat16))
    return stacks


def prolong_table(total, count, low, high, from_low, from_high, shape):
    own = total // count
    stack = []
    for place in range(count):
        i = np.arange(-low, own + high)[:, None]
        coarse = np.arange(-from_low, own // 2 + from_high)[None, :]
        where = i + place * own
        table = phi(i - 2 * coarse) * ((where >= 0) & (where < total))
        whole = np.zeros(shape)
        whole[: table.shape[0], : table.shape[1]] = table
        stack.append(whole)
    return np.stack(stack)


def shift(value, name, step):
    count = lax.axis_size(name)
    return lax.ppermute(value, name, [(i, (i + step) % count) for i in range(count)])


def split(x):
    high = x.astype(BF16)
    return high, (x - high.astype(F32)).astype(BF16)


def dot(a, b, dims=NN):
    return lax.dot_general(a, b, dims, preferred_element_type=F32)


def mm(a, b):
    a_high, a_low = split(a)
    b_high, b_low = split(b)
    return dot(a_high, b_high) + (dot(a_low, b_high) + dot(a_high, b_low))


def exact_left(table, x):
    high, low = split(x)
    return dot(table, high) + dot(table, low)


def exact_right(x, table):
    high, low = split(x)
    return dot(high, table) + dot(low, table)


def neighbours(name):
    place = lax.axis_index(name)
    count = lax.axis_size(name)
    return (place > 0).astype(F32), (place < count - 1).astype(F32)


def call(body, outs, us, in_specs, out_specs, after=(), carry=(), vmem=8, **kwargs):
    count, kept = len(in_specs), len(outs)
    total = count + len(after) + len(carry)
    shapes = [jax.ShapeDtypeStruct(s, F32) for s in outs]
    shapes += [jax.ShapeDtypeStruct(a.shape, a.dtype) for a in carry]

    def run(*refs):
        inner = refs[total:]
        body(*refs[:count], *inner[:kept], *inner[kept + len(carry) :])

    kernel = pl.pallas_call(
        run,
        out_shape=shapes,
        in_specs=[*in_specs, *[ANY] * (total - count)],
        out_specs=[*out_specs, *[ANY] * len(carry)],
        input_output_aliases={count + len(after) + k: kept + k for k in range(len(carry))},
        compiler_params=pltpu.CompilerParams(vmem_limit_bytes=vmem * 1024 * 1024),
        cost_estimate=pl.CostEstimate(
            flops=int(us * 1.15e10), bytes_accessed=int(us * 3.6e8), transcendentals=0
        ),
        **kwargs,
    )
    return lambda *args: kernel(*args, *after, *carry)


def grid_of(rows, cols):
    shape = (rows, cols)
    return lax.broadcasted_iota(jnp.int32, shape, 0), lax.broadcasted_iota(jnp.int32, shape, 1)


def lane_of(rows):
    return grid_of(rows, 128)[1]


def pack(first, second):
    return jnp.where(grid_of(8, 128)[0] < 4, first, second)


def unpack_low(tile, part):
    tile = tile if part else pltpu.roll(tile, 4, 0)
    return jnp.where(grid_of(8, 128)[0] >= 4, tile, 0.0)


def unpack_high(tile, part):
    tile = pltpu.roll(tile, 4, 0) if part else tile
    return jnp.where(grid_of(8, 128)[0] < 4, tile, 0.0)


def along_z(taps, count, first, last, load):
    planes = {}

    def get(i):
        if not 0 <= i < count:
            return None
        if i not in planes:
            planes[i] = load(i)
        return planes[i]

    for k in range(first, last + 1):
        total = None
        for d in range(9):
            below, above = get(k - d), (get(k + d) if d else None)
            pair = below if above is None else above if below is None else below + above
            if pair is None:
                continue
            pair = pair * taps[d]
            total = pair if total is None else total + pair
        yield k, total


def coarse_z_body(g, own1, own2, low, high):
    has_low, has_high = neighbours("gz")

    @pl.loop(0, 16)
    def _(chunk):
        rows = pl.ds(pl.multiple_of(8 * chunk, 8), 8)

        def weigh(at, count, get, low_at=0):
            total = None
            for offsets, weight in (((0,), 1.0), ((-1, 1), 0.5625), ((-3, 3), -0.0625)):
                part = None
                for o in offsets:
                    if low_at <= 2 * at + o < count:
                        value = get(2 * at + o)
                        part = value if part is None else part + value
                if part is not None:
                    part = part if weight == 1.0 else part * weight
                    total = part if total is None else total + part
            return total

        planes = {}

        def get(i):
            if i not in planes:
                planes[i] = g[i, rows, :]
            return planes[i]

        first = {}
        for j in range(-1, 34):
            first[j] = weigh(j, 64, get)
            if 0 <= j < 32:
                own1[j, rows, :] = first[j]
        for j, has in ((-1, has_low), (32, has_high), (33, has_high)):
            first[j] = first[j] * has
        low[0, rows, :] = first[-1]
        high[0, rows, :] = first[32]
        high[1, rows, :] = first[33]
        for k in range(-2, 19):
            value = weigh(k, 34, lambda j: first[j], -1)
            if k < 0:
                low[3 + k, rows, :] = value * has_low
            elif k < 16:
                own2[k, rows, :] = value
            else:
                high[k - 14, rows, :] = value * has_high


def coarse_z(g):
    return call(
        coarse_z_body,
        [(32, 128, 128), (16, 128, 128), (3, 128, 128), (5, 128, 128)],
        us=1.5,
        vmem=16,
        in_specs=[VMEM],
        out_specs=[VMEM] * 4,
    )(g)


def coarse_x_body(table, own1, own2, from_high, from_low, out1, out2, low, high):
    own_table = table[lax.axis_index("gx")]
    doubled = jnp.concatenate([own_table, own_table], axis=1)

    def work(source, out, at, pair, first, rows, extra=(None, None)):
        values = [source[2 * pair + k] for k in range(2)]
        values = [v if e is None else v + e for v, e in zip(values, extra)]
        wide = jnp.concatenate(split(jnp.concatenate(values, axis=0)), axis=1)
        full = dot(doubled[first : first + rows + 16], wide, NT)
        left, right = full[:, 0:128], full[:, 128:256]
        out[2 * pair] = left[:rows]
        out[2 * pair + 1] = right[:rows]
        low[at + pair] = pack(left[rows : rows + 8], right[rows : rows + 8])
        high[at + pair] = pack(left[rows + 8 :], right[rows + 8 :])

    for pair in range(16):
        extra = [from_low[0], from_low[1]] if pair == 0 else [None, None]
        if pair == 15:
            extra = [None, from_high[0]]
        work(own1, out1, 0, pair, 0, 64, extra)
    for pair in range(8):
        extra = [from_low[2], from_low[3]] if pair == 0 else [None, None]
        if pair == 1:
            extra = [from_low[4], None]
        if pair == 7:
            extra = [from_high[1], from_high[2]]
        work(own2, out2, 16, pair, 80, 32, extra)


def coarse_x(table, own1, own2, from_high, from_low, carry):
    return call(
        coarse_x_body,
        [(32, 64, 128), (16, 32, 128), (24, 8, 128), (24, 8, 128)],
        us=2,
        vmem=16,
        in_specs=[VMEM] * 5,
        out_specs=[VMEM] * 4,
        carry=carry,
    )(table, own1, own2, from_high, from_low)


def stacked(own, from_low, from_high, first, planes):
    parts = []
    for k in range(planes):
        z = first + k
        at, part = divmod(z, 2)
        rows = own.shape[1]
        parts.append(own[z, 0:8] + unpack_high(from_low[at], part))
        parts.append(own[z, 8 : rows - 8])
        parts.append(own[z, rows - 8 : rows] + unpack_low(from_high[at], part))
    return jnp.concatenate(parts, axis=0)


def mm_turned(table, value):
    t_high, t_low = split(table)
    high, low = split(value)
    wide = jnp.concatenate([t_high, t_low, t_high], axis=1)
    return dot(wide, jnp.concatenate([high, high, low], axis=1), NT)


def top_y_body(table, table1, own1, own2, from_high, from_low, top, near, near1, up, down, far):
    half = from_low.at[16:24], from_high.at[16:24]
    full = mm_turned(table[...], stacked(own2, *half, 0, 16))
    top[...] = full[0:24]
    up[0:24] = full[24:48]
    far[...] = full[48:72]
    down[0:24] = full[72:96]
    near[...] = full[96:136]
    down[24:40] = full[136:152]
    up[24:40] = full[152:168]
    for q in range(8):
        full = mm_turned(table1[...], stacked(own1, from_low, from_high, 4 * q, 4))
        near1[:, 256 * q : 256 * q + 256] = full[0:72]
        lanes = slice(256 * (q % 2), 256 * (q % 2) + 256)
        rows = slice(40 + 16 * (q // 2), 56 + 16 * (q // 2))
        down[rows, lanes] = full[72:88]
        up[rows, lanes] = full[88:104]


def top_y(table, table1, own1, own2, from_high, from_low, carry):
    return call(
        top_y_body,
        [(24, 512), (40, 512), (72, 2048), (104, 512), (104, 512), (24, 512)],
        us=1.5,
        in_specs=[VMEM] * 6,
        out_specs=[VMEM] * 6,
        carry=carry,
    )(table, table1, own1, own2, from_high, from_low)


def top_x_body(
    ttable, ntable, table1, edges, top, near, near1, f_low, f_high, f_far,
    otop, onear, onear1, up, down, far,
):
    total = top[...] + f_low[0:24] + (f_high[0:24] + f_far[...])
    extended = jnp.concatenate(
        [near[0:16] + f_low[24:40], near[16:24], near[24:40] + f_high[24:40]], axis=0
    )
    stacked = jnp.concatenate([total[:, 128 * t : 128 * t + 128] for t in range(4)], axis=0)
    full = mm(stacked, ttable[...])
    otop[...] = full[:, 0:128]
    up[0:96] = full[:, 128:256]
    far[...] = full[:, 256:384]
    down[0:96] = full[:, 384:512]
    stacked = jnp.concatenate([extended[:, 128 * t : 128 * t + 128] for t in range(4)], axis=0)
    full = mm(stacked, ntable[...])
    onear[...] = full[:, 0:256]
    down[96:256] = full[:, 256:384]
    up[96:256] = full[:, 384:512]
    tiles = []
    for t in range(16):
        lanes = slice(128 * t, 128 * t + 128)
        rows = slice(40 + 16 * (t // 4), 56 + 16 * (t // 4))
        part = slice(128 * (t % 4), 128 * (t % 4) + 128)
        parts = [near1[0:16, lanes] + f_low[rows, part], near1[16:56, lanes]]
        parts.append(near1[56:72, lanes] + f_high[rows, part])
        tiles.append(jnp.concatenate(parts, axis=0))
    for q in range(4):
        full = mm(jnp.concatenate(tiles[4 * q : 4 * q + 4], axis=1), edges[...])
        down[256 + 72 * q : 328 + 72 * q] = full[:, 0:128]
        up[256 + 72 * q : 328 + 72 * q] = full[:, 128:256]
    for t in range(16):
        full = mm(tiles[t], table1[...])
        onear1[2 * t] = full[:, 0:128]
        onear1[2 * t + 1] = full[:, 128:256]


def top_x(ttable, ntable, table1, edges, top, near, near1, f_low, f_high, f_far, after):
    return call(
        top_x_body,
        [(96, 128), (160, 256), (32, 72, 128), (544, 128), (544, 128), (96, 128)],
        us=2,
        in_specs=[VMEM] * 10,
        out_specs=[VMEM] * 6,
        after=after,
    )(ttable, ntable, table1, edges, top, near, near1, f_low, f_high, f_far)


def folded(values):
    lane = lane_of(values[0].shape[0])
    tail = jnp.zeros_like(values[0])
    for k, value in enumerate(values):
        tail = jnp.where(lane // 4 == k, pltpu.roll(value, (64 + 4 * k) % 128, 1), tail)
    packed = []
    for k in range(0, len(values), 2):
        second = pltpu.roll(values[k + 1], 64, 1) if k + 1 < len(values) else jnp.zeros_like(tail)
        packed.append(jnp.where(lane < 64, values[k], second))
    return [*packed, tail]


def unfold(buffer, k, tail):
    first = buffer[72 * (k // 2) : 72 * (k // 2) + 72]
    lane = lane_of(72)
    first = pltpu.roll(first, 64, 1) if k % 2 else first
    last = pltpu.roll(buffer[72 * tail : 72 * tail + 72], (64 - 4 * k) % 128, 1)
    return jnp.where(lane < 64, first, jnp.where(lane < 68, last, 0.0))


def one_z(taps, ext, from_high, from_low, out, up, down):
    has_low, has_high = neighbours("gz")
    weights = [taps[1, d] * 0.5 for d in range(9)]
    group = lane_of(8) // 16

    @pl.loop(0, 9)
    def _(chunk):
        rows = pl.ds(pl.multiple_of(8 * chunk, 8), 8)

        def load(z):
            q, g = z // 8, z % 8
            at = pl.ds(pl.multiple_of(256 + 72 * q + 8 * chunk, 8), 8)
            a = jnp.where(group == g, from_low[at, :], 0.0)
            b = jnp.where(group == g, from_high[at, :], 0.0)
            if g:
                a = pltpu.roll(a, 128 - 16 * g, 1)
            b = pltpu.roll(b, (57 - 16 * g) % 128, 1)
            return ext[z, rows, :] + (a + b)

        lows, highs = [], []
        for k, total in along_z(weights, 32, -8, 39, load):
            if k < 2:
                lows.append(total * has_low)
            if k > 30:
                highs.append(total * has_high)
            if -1 <= k < 34:
                out[k + 1, rows, :] = total * (has_low if k < 0 else has_high if k > 31 else 1.0)
        for values, buffer in ((lows, down), (highs, up)):
            for k, value in enumerate(folded(values)):
                buffer[pl.ds(pl.multiple_of(72 * k + 8 * chunk, 8), 8), :] = value


def top_z_body(
    taps, tcoef, ncoef, top, near, ext, f_low, f_high, f_far, parts, partner, onear, out1, up, down
):
    total = top[...] + f_low[0:96] + (f_high[0:96] + f_far[...])
    group = lane_of(24) // 32
    planes = []
    for z in range(16):
        tile = total[24 * (z // 4) : 24 * (z // 4) + 24]
        part = jnp.where(group == z % 4, tile, 0.0)
        part = part + pltpu.roll(part, 32, 1)
        planes.append(part + pltpu.roll(part, 64, 1))
    for step in range(8):
        out = partner if step // 4 else parts
        for quarter in range(4):
            value = None
            for z in range(16):
                at = (step * 4 + quarter) * 16 + z
                part = planes[z] * tcoef[at : at + 1, :]
                value = part if value is None else value + part
            rows = 96 * (step % 4) + 24 * quarter
            out[rows : rows + 24] = value
    lane = lane_of(40)
    planes = []
    for z in range(16):
        tile, q = z // 4, z % 4
        rows = slice(40 * tile, 40 * tile + 40)
        part = near[rows, 128 * (q // 2) : 128 * (q // 2) + 128]
        part = jnp.where(lane // 64 == q % 2, part, 0.0)
        low = jnp.where(lane // 32 == q, f_low[96 + 40 * tile : 136 + 40 * tile], 0.0)
        high = jnp.where(lane // 32 == q, f_high[96 + 40 * tile : 136 + 40 * tile], 0.0)
        if q % 2:
            part = pltpu.roll(part, 64, 1)
        if q:
            low = pltpu.roll(low, 128 - 32 * q, 1)
        high = pltpu.roll(high, (26 - 32 * q) % 128, 1)
        part = part + (low + high)
        planes.append(part + pltpu.roll(part, 64, 1))
    for out, base, count, first, offset in (
        (onear, 0, 11, -2, 0),
        (down, 11, 6, -8, 432),
        (up, 17, 5, 14, 432),
    ):
        for p in range(count):
            value = None
            for z in range(16):
                r = first + 2 * p
                if min(abs(r - z), abs(r + 1 - z)) > 8:
                    continue
                at = (base + p) * 16 + z
                part = planes[z] * ncoef[at : at + 1, :]
                value = part if value is None else value + part
            out[offset + 40 * p : offset + 40 * p + 40] = value

    one_z(taps, ext, f_high, f_low, out1, up, down)


def top_z(taps, tcoef, ncoef, top, near, ext, f_low, f_high, f_far, after):
    return call(
        top_z_body,
        [(384, 128), (384, 128), (440, 128), (35, 72, 128), (632, 128), (672, 128)],
        us=4,
        in_specs=[SMEM] + [VMEM] * 8,
        out_specs=[VMEM] * 6,
        after=after,
    )(taps, tcoef, ncoef, top, near, ext, f_low, f_high, f_far)


def top_sum_body(own, other, *outs):
    for k, out in enumerate(outs):
        rows = slice(96 * k, 96 * k + 96)
        out[...] = own[rows] + other[rows]


def top_sum(own, other, after):
    return call(
        top_sum_body,
        [(96, 128)] * 4,
        us=0.3,
        in_specs=[VMEM] * 2,
        out_specs=[VMEM] * 4,
        after=after,
    )(own, other)


def rise_body(
    py2, px2, mask2, py1, px1, mask1, py0, px0, top, p1, p2, p3, near2, f_low, f_high,
    near1, out, middle,
):
    z, y, x = [lax.axis_index(name) for name in AXES]
    py2, py1, py0 = py2[y], py1[y], py0[y]
    px2, px1, px0 = px2[x], px1[x], px0[x]
    total = (top[...] + p1[...]) + (p2[...] + p3[...])
    lane = lane_of(40)
    wide = jnp.concatenate([total[24 * q : 24 * q + 24] for q in range(4)], axis=1)
    tile = exact_left(py2, wide)
    rows = jnp.concatenate([tile[:, 128 * q : 128 * q + 128] for q in range(4)], axis=0)
    rows = exact_right(rows, px2)
    two = []
    for k in range(13):
        q, g = divmod(k, 4)
        part = rows[40 * q : 40 * q + 40, 128 * (g // 2) : 128 * (g // 2) + 128]
        part = jnp.where(lane // 64 == g % 2, part, 0.0)
        two.append(part + pltpu.roll(part, 64, 1))
    values = []
    for p in range(11):
        even = two[p + 1]
        if p < 10:
            odd = 0.5625 * (two[p + 1] + two[p + 2]) - 0.0625 * (two[p] + two[p + 3])
        else:
            odd = jnp.zeros_like(even)
        value = jnp.where(lane < 64, even, odd) * mask2[z, p : p + 1, :]
        value = value + near2[40 * p : 40 * p + 40]
        if p < 5:
            value = value + f_low[432 + 40 * p : 472 + 40 * p]
        else:
            value = value + f_high[432 + 40 * (p - 5) : 472 + 40 * (p - 5)]
        values.append(value)
    tile = exact_left(py1, jnp.concatenate(values, axis=1))
    rows = jnp.concatenate([tile[:, 128 * p : 128 * p + 128] for p in range(11)], axis=0)
    rows = exact_right(rows, px1)
    one = []
    for p in range(11):
        one.append(rows[72 * p : 72 * p + 72, 0:128])
        one.append(rows[72 * p : 72 * p + 72, 128:256])
    for f in range(35):
        if f % 2:
            value = one[(f + 3) // 2]
        else:
            h = f // 2
            value = 0.5625 * (one[h + 1] + one[h + 2]) - 0.0625 * (one[h] + one[h + 3])
        value = value * mask1[z, f] + near1[f]
        if f < 9:
            value = value + unfold(f_low, f, 5)
        elif f > 24:
            value = value + unfold(f_high, f - 25, 5)
        middle[72 * f : 72 * f + 72] = value
    doubled = jnp.concatenate([px0, px0], axis=0)
    left = jnp.concatenate([py0, py0], axis=1)
    for group in range(5):
        part = middle[504 * group : 504 * group + 504]
        part = dot(jnp.concatenate(split(part), axis=1), doubled)
        wide = jnp.concatenate([part[72 * k : 72 * k + 72] for k in range(7)], axis=1)
        full = dot(left, jnp.concatenate(split(wide), axis=0))
        for k in range(7):
            out[7 * group + k] = full[:, 128 * k : 128 * k + 128]


def rise(tables, top, others, near2, f_low, f_high, near1):
    return call(
        rise_body,
        [(35, 128, 128)],
        us=5,
        in_specs=[VMEM] * 5 + [SMEM] + [VMEM] * 10,
        out_specs=[VMEM],
        scratch_shapes=[pltpu.VMEM((2520, 128), F32)],
    )(*tables, top, *others, near2, f_low, f_high, near1)[0]


def near_z_body(taps, g, own, low, high):
    has_low, has_high = neighbours("gz")
    weights = [taps[0, d] for d in range(9)]

    @pl.loop(0, 16)
    def _(chunk):
        rows = pl.ds(pl.multiple_of(8 * chunk, 8), 8)
        for k, total in along_z(weights, 64, -8, 71, lambda i: g[i, rows, :]):
            if k < 0:
                low[k + 8, rows, :] = total * has_low
            elif k < 64:
                own[k, rows, :] = total
            else:
                high[k - 64, rows, :] = total * has_high


def near_z(taps, g, after):
    return call(
        near_z_body,
        [(64, 128, 128), (8, 128, 128), (8, 128, 128)],
        us=6,
        vmem=16,
        in_specs=[SMEM, VMEM],
        out_specs=[VMEM] * 3,
        after=after,
    )(taps, g)


def taps_at(taps, level, dist):
    value = jnp.zeros(dist.shape, F32)
    for d in range(9):
        value = jnp.where(dist == d, taps[level, d], value)
    return value


def near_at(taps, dist):
    return taps_at(taps, 0, jnp.abs(dist))


def near_x_body(taps, g, from_high, from_low, own, low, high):
    has_low, has_high = neighbours("gx")
    row, col = grid_of(128, 128)
    edge = near_at(taps, row - col + 8) * jnp.where(col < 8, has_low, 0.0)
    edge = edge + near_at(taps, row - col - 120) * jnp.where((col >= 8) & (col < 16), has_high, 0.0)
    upper, lower = split(jnp.concatenate([near_at(taps, row - col), edge], axis=1))
    table = jnp.concatenate([upper, upper], axis=0)

    def work(k, q, j, extra=None):
        value = g[k] if extra is None else g[k] + extra
        first, second = split(value)
        full = dot(jnp.concatenate([first, second], axis=1), table) + dot(first, lower)
        own[k] = full[:, 0:128]
        low[q, :, 8 * j : 8 * j + 8] = full[:, 128:136]
        high[q, :, 8 * j : 8 * j + 8] = full[:, 136:144]

    for j in range(16):
        work(j, 0, j, from_low[j] if j < 8 else None)

    @pl.loop(1, 3)
    def _(q):
        for j in range(16):
            work(16 * q + j, q, j)

    for j in range(16):
        work(48 + j, 3, j, from_high[j - 8] if j >= 8 else None)


def near_x(taps, g, from_high, from_low, after):
    return call(
        near_x_body,
        [(64, 128, 128), (4, 128, 128), (4, 128, 128)],
        us=5,
        vmem=16,
        in_specs=[SMEM] + [VMEM] * 3,
        out_specs=[VMEM] * 3,
        after=after,
    )(taps, g, from_high, from_low)


def near_y_body(taps, g, from_high, from_low, own, low, high):
    has_low, has_high = neighbours("gy")
    row, col = grid_of(8, 128)
    value = jnp.concatenate(
        [
            near_at(taps, grid_of(128, 128)[0] - grid_of(128, 128)[1]),
            near_at(taps, row - col - 8) * has_low,
            near_at(taps, row - col + 128) * has_high,
        ],
        axis=0,
    )
    upper, lower = split(value)
    wide_table = jnp.concatenate([upper, upper], axis=1)
    lane = lane_of(128)

    def load(q, j):
        left = pltpu.roll(from_low[q], (128 - 8 * j) % 128, 1)
        right = pltpu.roll(from_high[q], (120 - 8 * j) % 128, 1)
        sides = jnp.where(lane < 8, left, jnp.where(lane >= 120, right, 0.0))
        return g[16 * q + j] + sides

    @pl.loop(0, 4)
    def _(q):
        for pair in range(8):
            values = [load(q, 2 * pair + k) for k in range(2)]
            first, second = split(jnp.concatenate(values, axis=1))
            full = dot(wide_table, jnp.concatenate([first, second], axis=0))
            full = full + dot(lower, first)
            for k in range(2):
                at = 16 * q + 2 * pair + k
                part = full[:, 128 * k : 128 * k + 128]
                own[at] = part[0:128]
                low[at] = part[128:136]
                high[at] = part[136:144]


def near_y(taps, g, from_high, from_low, after):
    return call(
        near_y_body,
        [(64, 128, 128), (64, 8, 128), (64, 8, 128)],
        us=4,
        vmem=16,
        in_specs=[SMEM] + [VMEM] * 3,
        out_specs=[VMEM] * 3,
        after=after,
    )(taps, g, from_high, from_low)


def finest_body(near, from_high, from_low, coarse, out):
    step = pl.program_id(0)
    at = 8 * step
    planes = [coarse[at + h] for h in range(11)]
    for k in range(16):
        h = k // 2
        value = planes[h + 1]
        if k % 2:
            value = 0.5625 * (value + planes[h + 2]) - 0.0625 * (planes[h] + planes[h + 3])
        value = value + near[16 * step + k]
        out[k, 0:8] = value[0:8] + from_low[16 * step + k]
        out[k, 8:120] = value[8:120]
        out[k, 120:128] = value[120:128] + from_high[16 * step + k]


def finest(near, from_high, from_low, coarse):
    return call(
        finest_body,
        [(64, 128, 128)],
        us=4,
        vmem=16,
        grid=(4,),
        in_specs=[VMEM] * 4,
        out_specs=[pl.BlockSpec((16, 128, 128), lambda i: (i, 0, 0))],
    )(near, from_high, from_low, coarse)[0]


def phi_at(dist):
    dist = jnp.abs(dist)
    return jnp.where(
        dist == 0, 1.0, jnp.where(dist == 1, 0.5625, jnp.where(dist == 3, -0.0625, 0.0))
    ).astype(F32)


def toeplitz(line, rows, offset):
    line = pltpu.roll(line, lax.rem(192 - offset, 128), 1)
    wide = jnp.broadcast_to(line[0:1], (rows, 128))
    return pltpu.roll(wide, 0, 1, stride=1, stride_axis=0)


def tables_body(taps, top_taps, rows1, rows2, ytab, ttab, ntab, tcoef, ncoef, oney, onex, edges):
    z, y, x = [lax.axis_index(name) for name in AXES]
    dist = jnp.abs(lane_of(8) - 64)
    line = jnp.zeros((8, 128), F32)
    for d in range(64):
        line = jnp.where(dist == d, top_taps[d], line)

    def inside(r, place, own, total):
        where = r + place * own
        return (where >= 0) & (where < total)

    def near(level, dist, keep):
        return jnp.where(keep, taps_at(taps, level, jnp.abs(dist)), 0.0)

    second = rows2[y]
    j, c = grid_of(128, 48)
    keep = (j < 64) & (c < 37) & inside(c - 2, y, 32, 128)
    right = jnp.where(keep, phi_at(y * 32 + c - 2 - 2 * j), 0.0).astype(BF16)
    for s in range(4):
        first = lax.rem(y + s, 4) * 16 - 2
        left = toeplitz(line, 24, -first)
        i, l = grid_of(24, 128)
        keep = (l < 64) & (i < 21) & (first + i >= 0) & (first + i < 64)
        full = exact_right(jnp.where(keep, left, 0.0), right)
        ytab[24 * s : 24 * s + 24, :] = exact_right(full, second)
    i, c = grid_of(72, 48)
    keep = (i < 37) & inside(i - 2, y, 32, 128)
    keep = keep | ((i >= 40) & (i < 53) & (y > 0)) | ((i >= 56) & (i < 69) & (y < 3))
    r = jnp.where(i < 40, i - 2, jnp.where(i < 56, i - 50, i - 26))
    ytab[96:168, :] = exact_right(near(2, r - (c - 2), keep), second)

    i, l = grid_of(128, 64)
    left = phi_at(x * 32 + i % 32 - 2 * l).astype(BF16)
    i, l = grid_of(64, 128)
    a, b = grid_of(128, 128)
    for s in range(4):
        first = lax.rem(x + s, 4) * 16 - 2
        right = toeplitz(line, 64, first)
        keep = (l < 21) & (first + l >= 0) & (first + l < 64)
        right = jnp.where(keep, right, 0.0)
        right = right + pltpu.roll(right, 32, 1)
        right = right + pltpu.roll(right, 64, 1)
        full = exact_left(left, right)
        ttab[:, 128 * s : 128 * s + 128] = jnp.where(a // 32 == b // 32, full, 0.0)
    i, l = grid_of(128, 256)
    r = l % 64 - 2
    keep = (l // 64 == i // 32) & (l % 64 < 37) & inside(r, x, 32, 128)
    ntab[:, 0:256] = near(2, r - i % 32, keep)
    i, l = grid_of(128, 128)
    same = l // 32 == i // 32
    ntab[:, 256:384] = near(2, l % 32 - 8 - i % 32, same & (l % 32 < 11) & (x > 0))
    ntab[:, 384:512] = near(2, l % 32 + 30 - i % 32, same & (l % 32 < 10) & (x < 3))

    i, l = grid_of(16, 64)
    left = phi_at(z * 16 + i - 2 * l).astype(BF16)
    i, l = grid_of(64, 128)
    parts = []
    for s in range(8):
        chip, core = lax.rem(z // 2 + s % 4, 4), lax.rem(z + s // 4, 2)
        first = (2 * chip + core) * 8 - 2
        right = toeplitz(line, 64, first)
        keep = (l < 13) & (first + l >= 0) & (first + l < 64)
        parts.append(exact_left(left, jnp.where(keep, right, 0.0)))
    whole = jnp.concatenate(parts, axis=0) * 0.125
    i, l = grid_of(128, 128)
    for quarter in range(4):
        spread = jnp.where(i == 4 * quarter + l // 32, 1.0, 0.0).astype(BF16)
        full = exact_right(whole, spread)
        for s in range(8):
            at = (s * 4 + quarter) * 16
            tcoef[at : at + 16, :] = full[16 * s : 16 * s + 16]
    i, l = grid_of(16, 128)
    g = l // 64
    for p in range(22):
        if p < 11:
            r = g + (2 * p - 2)
            keep = (r <= 18) & inside(r, z, 16, 128)
        elif p < 17:
            r = g + (2 * (p - 11) - 8)
            keep = (r <= 2) & (z > 0)
        else:
            r = g + (2 * (p - 17) + 14)
            keep = (r <= 23) & (z < 7)
        ncoef[16 * p : 16 * p + 16, :] = near(2, r - i, keep) * 0.25

    i, c = grid_of(104, 80)
    keep = (i < 67) & inside(i - 1, y, 64, 256)
    keep = keep | ((i >= 72) & (i < 83) & (y > 0)) | ((i >= 88) & (i < 99) & (y < 3))
    r = jnp.where(i < 72, i - 1, jnp.where(i < 88, i - 81, i - 25))
    oney[...] = exact_right(near(1, r - (c - 1), keep), rows1[y])
    i, l = grid_of(128, 256)
    r = l % 128 - 1
    keep = (l // 128 == i // 64) & (l % 128 < 67) & inside(r, x, 64, 256)
    onex[...] = near(1, r - i % 64, keep)
    i, l = grid_of(512, 128)
    same = l // 16 == i // 64
    edges[:, 0:128] = near(1, l % 16 - 8 - i % 64, same & (l % 16 < 10) & (x > 0))
    edges[:, 128:256] = near(1, l % 16 + 63 - i % 64, same & (l % 16 < 9) & (x < 3))


def tables(taps, top_taps, after):
    return call(
        tables_body,
        [
            (168, 128), (128, 512), (128, 512), (512, 128),
            (352, 128), (104, 128), (128, 256), (512, 256),
        ],
        us=2,
        in_specs=[SMEM, SMEM, VMEM, VMEM],
        out_specs=[VMEM] * 8,
        after=after,
    )(taps, top_taps, *[jnp.asarray(t) for t in chain_rows(512, 4)])


def rise_tables():
    def kron(table, groups):
        return np.stack([np.kron(np.eye(groups), t.T) for t in table])

    y2 = prolong_table(128, 4, 2, 3, 2, 3, (40, 24))
    x2 = kron(prolong_table(128, 4, 2, 3, 2, 3, (64, 32)), 4)
    y1 = prolong_table(256, 4, 1, 2, 2, 3, (72, 40))
    x1 = kron(prolong_table(256, 4, 1, 2, 2, 3, (128, 64)), 2)
    y0 = prolong_table(512, 4, 0, 0, 1, 2, (128, 72))
    x0 = kron(prolong_table(512, 4, 0, 0, 1, 2, (128, 128)), 1)
    mask2 = np.zeros((8, 11, 128), np.float32)
    mask1 = np.zeros((8, 35), np.float32)
    for place in range(8):
        for e in range(22):
            inside = 0 <= place * 16 - 2 + e < 128
            mask2[place, e // 2, 64 * (e % 2) : 64 * (e % 2) + 64] = inside
        for f in range(35):
            mask1[place, f] = 0 <= place * 32 - 1 + f < 256
    half = lambda table: jnp.asarray(table.astype(jnp.bfloat16))
    return half(y2), half(x2), jnp.asarray(mask2), half(y1), half(x1), jnp.asarray(mask1), half(y0), half(x0)


def per_device(charges, taps, top_taps):
    z, y, x = AXES
    chain = jnp.asarray(chain_tables(512, 4))

    one, two, low, high = coarse_z(charges)
    f_high, f_low = shift(low, z, -1), shift(high, z, 1)
    near, *nsides = near_z(taps, charges, (two,))
    nf_high, nf_low = shift(nsides[0], z, -1), shift(nsides[1], z, 1)
    ytab, ttab, ntab, tcoef, ncoef, oney, onex, edges = tables(taps, top_taps, (two,))

    one, two, low, high = coarse_x(chain, one, two, f_high, f_low, ())
    f_high, f_low = shift(low, x, -1), shift(high, x, 1)
    near, *nsides = near_x(taps, near, nf_high, nf_low, (two,))

    top, near2, near1, up, down, far, *nsides = top_y(ytab, oney, one, two, f_high, f_low, nsides)
    f_low, f_high, f_far = shift(up, y, 1), shift(down, y, -1), shift(far, y, 2)
    nf_high, nf_low = shift(nsides[0], x, -1), shift(nsides[1], x, 1)

    top, near2, near1, up, down, far = top_x(
        ttab, ntab, onex, edges, top, near2, near1, f_low, f_high, f_far, ()
    )
    f_low, f_high, f_far = shift(up, x, 1), shift(down, x, -1), shift(far, x, 2)
    near, *nsides = near_y(taps, near, nf_high, nf_low, (top,))

    top, partner, near2, near1, up, down = top_z(
        taps, tcoef, ncoef, top, near2, near1, f_low, f_high, f_far, (nsides[0],)
    )
    count = lax.axis_size(z)
    partner = lax.ppermute(partner, z, [(i, i ^ 1) for i in range(count)])
    f_low, f_high = shift(up, z, 1), shift(down, z, -1)
    nf_high, nf_low = shift(nsides[0], y, -1), shift(nsides[1], y, 1)
    top, *others = top_sum(top, partner, (nf_high, nf_low))
    others = [shift(part, z, 2 + 2 * k) for k, part in enumerate(others)]

    coarse = rise(rise_tables(), top, others, near2, f_low, f_high, near1)
    return finest(near, nf_high, nf_low, coarse)


def solution(mesh):
    return jax.shard_map(
        per_device,
        mesh=mesh,
        in_specs=(P("gz", "gy", "gx"), P(), P()),
        out_specs=P("gz", "gy", "gx"),
        check_vma=False,
    )
```

```python
import jax
import jax.numpy as jnp
import numpy as np
from jax import lax
from jax.experimental import pallas as pl
from jax.experimental.pallas import tpu as pltpu
from jax.sharding import PartitionSpec as P

AXES = ("gz", "gy", "gx")
F32 = jnp.float32
BF16 = jnp.bfloat16
NN = (((1,), (0,)), ((), ()))
NT = (((1,), (1,)), ((), ()))
ANY = pl.BlockSpec(memory_space=pl.ANY)
SMEM = pl.BlockSpec(memory_space=pltpu.SMEM)
VMEM = pl.BlockSpec(memory_space=pltpu.VMEM)


def phi(dist):
    dist = np.abs(dist)
    return np.where(
        dist == 0, 1.0, np.where(dist == 1, 0.5625, np.where(dist == 3, -0.0625, 0.0))
    )


def restrict_whole(size):
    rows = np.arange(size // 2)[:, None]
    cols = np.arange(size)[None, :]
    return phi(cols - 2 * rows)


def rows_of(whole, first, count):
    picked = np.zeros((count, whole.shape[1]))
    for r in range(count):
        if 0 <= first + r < whole.shape[0]:
            picked[r] = whole[first + r]
    return picked


def chain_tables(size, count):
    own0 = size // count
    first = restrict_whole(size)
    second = restrict_whole(size // 2) @ first
    stack = []
    for place in range(count):
        parts = []
        for whole, own, low, high in ((first, own0 // 2, 1, 2), (second, own0 // 4, 2, 3)):
            cols = whole[:, place * own0 : (place + 1) * own0]
            at = place * own
            parts.append(rows_of(cols, at, own))
            to_low = [np.zeros((4 - low, own0)), rows_of(cols, at - low, low)]
            to_high = [rows_of(cols, at + own, high), np.zeros((4 - high, own0))]
            parts.extend(to_low * 2 + to_high * 2)
        stack.append(np.concatenate(parts))
    return np.stack(stack).astype(jnp.bfloat16)


def chain_rows(size, count):
    own0 = size // count
    first = restrict_whole(size)
    second = restrict_whole(size // 2) @ first
    stacks = []
    for whole, own, low, high, rows in ((first, own0 // 2, 1, 2, 80), (second, own0 // 4, 2, 3, 48)):
        stack = np.zeros((count, rows, own0))
        for place in range(count):
            cols = whole[:, place * own0 : (place + 1) * own0]
            stack[place, : own + low + high] = rows_of(cols, place * own - low, own + low + high)
        stacks.append(stack.astype(jnp.bfloat16))
    return stacks


def prolong_table(total, count, low, high, from_low, from_high, shape):
    own = total // count
    stack = []
    for place in range(count):
        i = np.arange(-low, own + high)[:, None]
        coarse = np.arange(-from_low, own // 2 + from_high)[None, :]
        where = i + place * own
        table = phi(i - 2 * coarse) * ((where >= 0) & (where < total))
        whole = np.zeros(shape)
        whole[: table.shape[0], : table.shape[1]] = table
        stack.append(whole)
    return np.stack(stack)


def shift(value, name, step):
    count = lax.axis_size(name)
    return lax.ppermute(value, name, [(i, (i + step) % count) for i in range(count)])


def split(x):
    high = x.astype(BF16)
    return high, (x - high.astype(F32)).astype(BF16)


def dot(a, b, dims=NN):
    return lax.dot_general(a, b, dims, preferred_element_type=F32)


def mm(a, b):
    a_high, a_low = split(a)
    b_high, b_low = split(b)
    return dot(a_high, b_high) + (dot(a_low, b_high) + dot(a_high, b_low))


def exact_left(table, x):
    high, low = split(x)
    return dot(table, high) + dot(table, low)


def exact_right(x, table):
    high, low = split(x)
    return dot(high, table) + dot(low, table)


def neighbours(name):
    place = lax.axis_index(name)
    count = lax.axis_size(name)
    return (place > 0).astype(F32), (place < count - 1).astype(F32)


def call(body, outs, us, in_specs, out_specs, after=(), carry=(), vmem=8, **kwargs):
    count, kept = len(in_specs), len(outs)
    total = count + len(after) + len(carry)
    shapes = [jax.ShapeDtypeStruct(s, F32) for s in outs]
    shapes += [jax.ShapeDtypeStruct(a.shape, a.dtype) for a in carry]

    def run(*refs):
        inner = refs[total:]
        body(*refs[:count], *inner[:kept], *inner[kept + len(carry) :])

    kernel = pl.pallas_call(
        run,
        out_shape=shapes,
        in_specs=[*in_specs, *[ANY] * (total - count)],
        out_specs=[*out_specs, *[ANY] * len(carry)],
        input_output_aliases={count + len(after) + k: kept + k for k in range(len(carry))},
        compiler_params=pltpu.CompilerParams(vmem_limit_bytes=vmem * 1024 * 1024),
        cost_estimate=pl.CostEstimate(
            flops=int(us * 1.15e10), bytes_accessed=int(us * 3.6e8), transcendentals=0
        ),
        **kwargs,
    )
    return lambda *args: kernel(*args, *after, *carry)


def grid_of(rows, cols):
    shape = (rows, cols)
    return lax.broadcasted_iota(jnp.int32, shape, 0), lax.broadcasted_iota(jnp.int32, shape, 1)


def lane_of(rows):
    return grid_of(rows, 128)[1]


def pack(first, second):
    return jnp.where(grid_of(8, 128)[0] < 4, first, second)


def unpack_low(tile, part):
    tile = tile if part else pltpu.roll(tile, 4, 0)
    return jnp.where(grid_of(8, 128)[0] >= 4, tile, 0.0)


def unpack_high(tile, part):
    tile = pltpu.roll(tile, 4, 0) if part else tile
    return jnp.where(grid_of(8, 128)[0] < 4, tile, 0.0)


def along_z(taps, count, first, last, load):
    planes = {}

    def get(i):
        if not 0 <= i < count:
            return None
        if i not in planes:
            planes[i] = load(i)
        return planes[i]

    for k in range(first, last + 1):
        total = None
        for d in range(9):
            below, above = get(k - d), (get(k + d) if d else None)
            pair = below if above is None else above if below is None else below + above
            if pair is None:
                continue
            pair = pair * taps[d]
            total = pair if total is None else total + pair
        yield k, total


def coarse_z_body(g, own1, own2, low, high):
    has_low, has_high = neighbours("gz")

    @pl.loop(0, 16)
    def _(chunk):
        rows = pl.ds(pl.multiple_of(8 * chunk, 8), 8)

        def weigh(at, count, get, low_at=0):
            total = None
            for offsets, weight in (((0,), 1.0), ((-1, 1), 0.5625), ((-3, 3), -0.0625)):
                part = None
                for o in offsets:
                    if low_at <= 2 * at + o < count:
                        value = get(2 * at + o)
                        part = value if part is None else part + value
                if part is not None:
                    part = part if weight == 1.0 else part * weight
                    total = part if total is None else total + part
            return total

        planes = {}

        def get(i):
            if i not in planes:
                planes[i] = g[i, rows, :]
            return planes[i]

        first = {}
        for j in range(-1, 34):
            first[j] = weigh(j, 64, get)
            if 0 <= j < 32:
                own1[j, rows, :] = first[j]
        for j, has in ((-1, has_low), (32, has_high), (33, has_high)):
            first[j] = first[j] * has
        low[0, rows, :] = first[-1]
        high[0, rows, :] = first[32]
        high[1, rows, :] = first[33]
        for k in range(-2, 19):
            value = weigh(k, 34, lambda j: first[j], -1)
            if k < 0:
                low[3 + k, rows, :] = value * has_low
            elif k < 16:
                own2[k, rows, :] = value
            else:
                high[k - 14, rows, :] = value * has_high


def coarse_z(g):
    return call(
        coarse_z_body,
        [(32, 128, 128), (16, 128, 128), (3, 128, 128), (5, 128, 128)],
        us=1.5,
        vmem=16,
        in_specs=[VMEM],
        out_specs=[VMEM] * 4,
    )(g)


def coarse_x_body(table, own1, own2, from_high, from_low, out1, out2, low, high):
    own_table = table[lax.axis_index("gx")]
    doubled = jnp.concatenate([own_table, own_table], axis=1)

    def work(source, out, at, pair, first, rows, extra=(None, None)):
        values = [source[2 * pair + k] for k in range(2)]
        values = [v if e is None else v + e for v, e in zip(values, extra)]
        wide = jnp.concatenate(split(jnp.concatenate(values, axis=0)), axis=1)
        full = dot(doubled[first : first + rows + 16], wide, NT)
        left, right = full[:, 0:128], full[:, 128:256]
        out[2 * pair] = left[:rows]
        out[2 * pair + 1] = right[:rows]
        low[at + pair] = pack(left[rows : rows + 8], right[rows : rows + 8])
        high[at + pair] = pack(left[rows + 8 :], right[rows + 8 :])

    for pair in range(16):
        extra = [from_low[0], from_low[1]] if pair == 0 else [None, None]
        if pair == 15:
            extra = [None, from_high[0]]
        work(own1, out1, 0, pair, 0, 64, extra)
    for pair in range(8):
        extra = [from_low[2], from_low[3]] if pair == 0 else [None, None]
        if pair == 1:
            extra = [from_low[4], None]
        if pair == 7:
            extra = [from_high[1], from_high[2]]
        work(own2, out2, 16, pair, 80, 32, extra)


def coarse_x(table, own1, own2, from_high, from_low, carry):
    return call(
        coarse_x_body,
        [(32, 64, 128), (16, 32, 128), (24, 8, 128), (24, 8, 128)],
        us=2,
        vmem=16,
        in_specs=[VMEM] * 5,
        out_specs=[VMEM] * 4,
        carry=carry,
    )(table, own1, own2, from_high, from_low)


def stacked(own, from_low, from_high, first, planes):
    parts = []
    for k in range(planes):
        z = first + k
        at, part = divmod(z, 2)
        rows = own.shape[1]
        parts.append(own[z, 0:8] + unpack_high(from_low[at], part))
        parts.append(own[z, 8 : rows - 8])
        parts.append(own[z, rows - 8 : rows] + unpack_low(from_high[at], part))
    return jnp.concatenate(parts, axis=0)


def mm_turned(table, value):
    t_high, t_low = split(table)
    high, low = split(value)
    wide = jnp.concatenate([t_high, t_low, t_high], axis=1)
    return dot(wide, jnp.concatenate([high, high, low], axis=1), NT)


def top_y_body(table, table1, own1, own2, from_high, from_low, top, near, near1, up, down, far):
    half = from_low.at[16:24], from_high.at[16:24]
    full = mm_turned(table[...], stacked(own2, *half, 0, 16))
    top[...] = full[0:24]
    up[0:24] = full[24:48]
    far[...] = full[48:72]
    down[0:24] = full[72:96]
    near[...] = full[96:136]
    down[24:40] = full[136:152]
    up[24:40] = full[152:168]
    for q in range(8):
        full = mm_turned(table1[...], stacked(own1, from_low, from_high, 4 * q, 4))
        near1[:, 256 * q : 256 * q + 256] = full[0:72]
        lanes = slice(256 * (q % 2), 256 * (q % 2) + 256)
        rows = slice(40 + 16 * (q // 2), 56 + 16 * (q // 2))
        down[rows, lanes] = full[72:88]
        up[rows, lanes] = full[88:104]


def top_y(table, table1, own1, own2, from_high, from_low, carry):
    return call(
        top_y_body,
        [(24, 512), (40, 512), (72, 2048), (104, 512), (104, 512), (24, 512)],
        us=1.5,
        in_specs=[VMEM] * 6,
        out_specs=[VMEM] * 6,
        carry=carry,
    )(table, table1, own1, own2, from_high, from_low)


def top_x_body(
    ttable, ntable, table1, edges, top, near, near1, f_low, f_high, f_far,
    otop, onear, onear1, up, down, far,
):
    total = top[...] + f_low[0:24] + (f_high[0:24] + f_far[...])
    extended = jnp.concatenate(
        [near[0:16] + f_low[24:40], near[16:24], near[24:40] + f_high[24:40]], axis=0
    )
    stacked = jnp.concatenate([total[:, 128 * t : 128 * t + 128] for t in range(4)], axis=0)
    full = mm(stacked, ttable[...])
    otop[...] = full[:, 0:128]
    up[0:96] = full[:, 128:256]
    far[...] = full[:, 256:384]
    down[0:96] = full[:, 384:512]
    stacked = jnp.concatenate([extended[:, 128 * t : 128 * t + 128] for t in range(4)], axis=0)
    full = mm(stacked, ntable[...])
    onear[...] = full[:, 0:256]
    down[96:256] = full[:, 256:384]
    up[96:256] = full[:, 384:512]
    tiles = []
    for t in range(16):
        lanes = slice(128 * t, 128 * t + 128)
        rows = slice(40 + 16 * (t // 4), 56 + 16 * (t // 4))
        part = slice(128 * (t % 4), 128 * (t % 4) + 128)
        parts = [near1[0:16, lanes] + f_low[rows, part], near1[16:56, lanes]]
        parts.append(near1[56:72, lanes] + f_high[rows, part])
        tiles.append(jnp.concatenate(parts, axis=0))
    for q in range(4):
        full = mm(jnp.concatenate(tiles[4 * q : 4 * q + 4], axis=1), edges[...])
        down[256 + 72 * q : 328 + 72 * q] = full[:, 0:128]
        up[256 + 72 * q : 328 + 72 * q] = full[:, 128:256]
    for t in range(16):
        full = mm(tiles[t], table1[...])
        onear1[2 * t] = full[:, 0:128]
        onear1[2 * t + 1] = full[:, 128:256]


def top_x(ttable, ntable, table1, edges, top, near, near1, f_low, f_high, f_far, after):
    return call(
        top_x_body,
        [(96, 128), (160, 256), (32, 72, 128), (544, 128), (544, 128), (96, 128)],
        us=2,
        in_specs=[VMEM] * 10,
        out_specs=[VMEM] * 6,
        after=after,
    )(ttable, ntable, table1, edges, top, near, near1, f_low, f_high, f_far)


def folded(values):
    lane = lane_of(values[0].shape[0])
    tail = jnp.zeros_like(values[0])
    for k, value in enumerate(values):
        tail = jnp.where(lane // 4 == k, pltpu.roll(value, (64 + 4 * k) % 128, 1), tail)
    packed = []
    for k in range(0, len(values), 2):
        second = pltpu.roll(values[k + 1], 64, 1) if k + 1 < len(values) else jnp.zeros_like(tail)
        packed.append(jnp.where(lane < 64, values[k], second))
    return [*packed, tail]


def unfold(buffer, k, tail):
    first = buffer[72 * (k // 2) : 72 * (k // 2) + 72]
    lane = lane_of(72)
    first = pltpu.roll(first, 64, 1) if k % 2 else first
    last = pltpu.roll(buffer[72 * tail : 72 * tail + 72], (64 - 4 * k) % 128, 1)
    return jnp.where(lane < 64, first, jnp.where(lane < 68, last, 0.0))


def one_z(taps, ext, from_high, from_low, out, up, down):
    has_low, has_high = neighbours("gz")
    weights = [taps[1, d] * 0.5 for d in range(9)]
    group = lane_of(8) // 16

    @pl.loop(0, 9)
    def _(chunk):
        rows = pl.ds(pl.multiple_of(8 * chunk, 8), 8)

        def load(z):
            q, g = z // 8, z % 8
            at = pl.ds(pl.multiple_of(256 + 72 * q + 8 * chunk, 8), 8)
            a = jnp.where(group == g, from_low[at, :], 0.0)
            b = jnp.where(group == g, from_high[at, :], 0.0)
            if g:
                a = pltpu.roll(a, 128 - 16 * g, 1)
            b = pltpu.roll(b, (57 - 16 * g) % 128, 1)
            return ext[z, rows, :] + (a + b)

        lows, highs = [], []
        for k, total in along_z(weights, 32, -8, 39, load):
            if k < 2:
                lows.append(total * has_low)
            if k > 30:
                highs.append(total * has_high)
            if -1 <= k < 34:
                out[k + 1, rows, :] = total * (has_low if k < 0 else has_high if k > 31 else 1.0)
        for values, buffer in ((lows, down), (highs, up)):
            for k, value in enumerate(folded(values)):
                buffer[pl.ds(pl.multiple_of(72 * k + 8 * chunk, 8), 8), :] = value


def top_z_body(
    taps, tcoef, ncoef, top, near, ext, f_low, f_high, f_far, parts, partner, onear, out1, up, down
):
    total = top[...] + f_low[0:96] + (f_high[0:96] + f_far[...])
    group = lane_of(24) // 32
    planes = []
    for z in range(16):
        tile = total[24 * (z // 4) : 24 * (z // 4) + 24]
        part = jnp.where(group == z % 4, tile, 0.0)
        part = part + pltpu.roll(part, 32, 1)
        planes.append(part + pltpu.roll(part, 64, 1))
    for step in range(8):
        out = partner if step // 4 else parts
        for quarter in range(4):
            value = None
            for z in range(16):
                at = (step * 4 + quarter) * 16 + z
                part = planes[z] * tcoef[at : at + 1, :]
                value = part if value is None else value + part
            rows = 96 * (step % 4) + 24 * quarter
            out[rows : rows + 24] = value
    lane = lane_of(40)
    planes = []
    for z in range(16):
        tile, q = z // 4, z % 4
        rows = slice(40 * tile, 40 * tile + 40)
        part = near[rows, 128 * (q // 2) : 128 * (q // 2) + 128]
        part = jnp.where(lane // 64 == q % 2, part, 0.0)
        low = jnp.where(lane // 32 == q, f_low[96 + 40 * tile : 136 + 40 * tile], 0.0)
        high = jnp.where(lane // 32 == q, f_high[96 + 40 * tile : 136 + 40 * tile], 0.0)
        if q % 2:
            part = pltpu.roll(part, 64, 1)
        if q:
            low = pltpu.roll(low, 128 - 32 * q, 1)
        high = pltpu.roll(high, (26 - 32 * q) % 128, 1)
        part = part + (low + high)
        planes.append(part + pltpu.roll(part, 64, 1))
    for out, base, count, first, offset in (
        (onear, 0, 11, -2, 0),
        (down, 11, 6, -8, 432),
        (up, 17, 5, 14, 432),
    ):
        for p in range(count):
            value = None
            for z in range(16):
                r = first + 2 * p
                if min(abs(r - z), abs(r + 1 - z)) > 8:
                    continue
                at = (base + p) * 16 + z
                part = planes[z] * ncoef[at : at + 1, :]
                value = part if value is None else value + part
            out[offset + 40 * p : offset + 40 * p + 40] = value

    one_z(taps, ext, f_high, f_low, out1, up, down)


def top_z(taps, tcoef, ncoef, top, near, ext, f_low, f_high, f_far, after):
    return call(
        top_z_body,
        [(384, 128), (384, 128), (440, 128), (35, 72, 128), (632, 128), (672, 128)],
        us=4,
        in_specs=[SMEM] + [VMEM] * 8,
        out_specs=[VMEM] * 6,
        after=after,
    )(taps, tcoef, ncoef, top, near, ext, f_low, f_high, f_far)


def top_sum_body(own, other, *outs):
    for k, out in enumerate(outs):
        rows = slice(96 * k, 96 * k + 96)
        out[...] = own[rows] + other[rows]


def top_sum(own, other, after):
    return call(
        top_sum_body,
        [(96, 128)] * 4,
        us=0.3,
        in_specs=[VMEM] * 2,
        out_specs=[VMEM] * 4,
        after=after,
    )(own, other)


def rise_body(
    py2, px2, mask2, py1, px1, mask1, py0, px0, top, p1, p2, p3, near2, f_low, f_high,
    near1, out, middle,
):
    z, y, x = [lax.axis_index(name) for name in AXES]
    py2, py1, py0 = py2[y], py1[y], py0[y]
    px2, px1, px0 = px2[x], px1[x], px0[x]
    total = (top[...] + p1[...]) + (p2[...] + p3[...])
    lane = lane_of(40)
    wide = jnp.concatenate([total[24 * q : 24 * q + 24] for q in range(4)], axis=1)
    tile = exact_left(py2, wide)
    rows = jnp.concatenate([tile[:, 128 * q : 128 * q + 128] for q in range(4)], axis=0)
    rows = exact_right(rows, px2)
    two = []
    for k in range(13):
        q, g = divmod(k, 4)
        part = rows[40 * q : 40 * q + 40, 128 * (g // 2) : 128 * (g // 2) + 128]
        part = jnp.where(lane // 64 == g % 2, part, 0.0)
        two.append(part + pltpu.roll(part, 64, 1))
    values = []
    for p in range(11):
        even = two[p + 1]
        if p < 10:
            odd = 0.5625 * (two[p + 1] + two[p + 2]) - 0.0625 * (two[p] + two[p + 3])
        else:
            odd = jnp.zeros_like(even)
        value = jnp.where(lane < 64, even, odd) * mask2[z, p : p + 1, :]
        value = value + near2[40 * p : 40 * p + 40]
        if p < 5:
            value = value + f_low[432 + 40 * p : 472 + 40 * p]
        else:
            value = value + f_high[432 + 40 * (p - 5) : 472 + 40 * (p - 5)]
        values.append(value)
    tile = exact_left(py1, jnp.concatenate(values, axis=1))
    rows = jnp.concatenate([tile[:, 128 * p : 128 * p + 128] for p in range(11)], axis=0)
    rows = exact_right(rows, px1)
    one = []
    for p in range(11):
        one.append(rows[72 * p : 72 * p + 72, 0:128])
        one.append(rows[72 * p : 72 * p + 72, 128:256])
    for f in range(35):
        if f % 2:
            value = one[(f + 3) // 2]
        else:
            h = f // 2
            value = 0.5625 * (one[h + 1] + one[h + 2]) - 0.0625 * (one[h] + one[h + 3])
        value = value * mask1[z, f] + near1[f]
        if f < 9:
            value = value + unfold(f_low, f, 5)
        elif f > 24:
            value = value + unfold(f_high, f - 25, 5)
        middle[72 * f : 72 * f + 72] = value
    doubled = jnp.concatenate([px0, px0], axis=0)
    left = jnp.concatenate([py0, py0], axis=1)
    for group in range(5):
        part = middle[504 * group : 504 * group + 504]
        part = dot(jnp.concatenate(split(part), axis=1), doubled)
        wide = jnp.concatenate([part[72 * k : 72 * k + 72] for k in range(7)], axis=1)
        full = dot(left, jnp.concatenate(split(wide), axis=0))
        for k in range(7):
            out[7 * group + k] = full[:, 128 * k : 128 * k + 128]


def rise(tables, top, others, near2, f_low, f_high, near1):
    return call(
        rise_body,
        [(35, 128, 128)],
        us=5,
        in_specs=[VMEM] * 5 + [SMEM] + [VMEM] * 10,
        out_specs=[VMEM],
        scratch_shapes=[pltpu.VMEM((2520, 128), F32)],
    )(*tables, top, *others, near2, f_low, f_high, near1)[0]


def near_z_body(taps, g, own, low, high):
    has_low, has_high = neighbours("gz")
    weights = [taps[0, d] for d in range(9)]

    @pl.loop(0, 16)
    def _(chunk):
        rows = pl.ds(pl.multiple_of(8 * chunk, 8), 8)
        for k, total in along_z(weights, 64, -8, 71, lambda i: g[i, rows, :]):
            if k < 0:
                low[k + 8, rows, :] = total * has_low
            elif k < 64:
                own[k, rows, :] = total
            else:
                high[k - 64, rows, :] = total * has_high


def near_z(taps, g, after):
    return call(
        near_z_body,
        [(64, 128, 128), (8, 128, 128), (8, 128, 128)],
        us=6,
        vmem=16,
        in_specs=[SMEM, VMEM],
        out_specs=[VMEM] * 3,
        after=after,
    )(taps, g)


def taps_at(taps, level, dist):
    value = jnp.zeros(dist.shape, F32)
    for d in range(9):
        value = jnp.where(dist == d, taps[level, d], value)
    return value


def near_at(taps, dist):
    return taps_at(taps, 0, jnp.abs(dist))


def near_x_body(taps, g, from_high, from_low, own, low, high):
    has_low, has_high = neighbours("gx")
    row, col = grid_of(128, 128)
    edge = near_at(taps, row - col + 8) * jnp.where(col < 8, has_low, 0.0)
    edge = edge + near_at(taps, row - col - 120) * jnp.where((col >= 8) & (col < 16), has_high, 0.0)
    upper, lower = split(jnp.concatenate([near_at(taps, row - col), edge], axis=1))
    table = jnp.concatenate([upper, upper], axis=0)

    def work(k, q, j, extra=None):
        value = g[k] if extra is None else g[k] + extra
        first, second = split(value)
        full = dot(jnp.concatenate([first, second], axis=1), table) + dot(first, lower)
        own[k] = full[:, 0:128]
        at = 8 * ((j - 1) % 16)
        low[q, :, at : at + 8] = full[:, 128:136]
        high[q, :, 8 * j : 8 * j + 8] = full[:, 136:144]

    for j in range(16):
        work(j, 0, j, from_low[j] if j < 8 else None)

    @pl.loop(1, 3)
    def _(q):
        for j in range(16):
            work(16 * q + j, q, j)

    for j in range(16):
        work(48 + j, 3, j, from_high[j - 8] if j >= 8 else None)


def near_x(taps, g, from_high, from_low, after):
    return call(
        near_x_body,
        [(64, 128, 128), (4, 128, 128), (4, 128, 128)],
        us=5,
        vmem=16,
        in_specs=[SMEM] + [VMEM] * 3,
        out_specs=[VMEM] * 3,
        after=after,
    )(taps, g, from_high, from_low)


def near_y_body(taps, g, from_high, from_low, own, low, high):
    has_low, has_high = neighbours("gy")
    row, col = grid_of(8, 128)
    value = jnp.concatenate(
        [
            near_at(taps, grid_of(128, 128)[0] - grid_of(128, 128)[1]),
            near_at(taps, row - col - 8) * has_low,
            near_at(taps, row - col + 128) * has_high,
        ],
        axis=0,
    )
    upper, lower = split(value)
    wide_table = jnp.concatenate([upper, upper], axis=1)
    lane = lane_of(128)

    def load(q, j):
        sides = jnp.where(lane // 8 == j, from_low[q], from_high[q])
        sides = pltpu.roll(sides, (128 - 8 * j) % 128, 1) if j else sides
        return g[16 * q + j] + jnp.where((lane < 8) | (lane >= 120), sides, 0.0)

    @pl.loop(0, 4)
    def _(q):
        for pair in range(8):
            values = [load(q, 2 * pair + k) for k in range(2)]
            first, second = split(jnp.concatenate(values, axis=1))
            full = dot(wide_table, jnp.concatenate([first, second], axis=0))
            full = full + dot(lower, first)
            for k in range(2):
                at = 16 * q + 2 * pair + k
                part = full[:, 128 * k : 128 * k + 128]
                own[at] = part[0:128]
                low[at] = part[128:136]
                high[at] = part[136:144]


def near_y(taps, g, from_high, from_low, after):
    return call(
        near_y_body,
        [(64, 128, 128), (64, 8, 128), (64, 8, 128)],
        us=4,
        vmem=16,
        in_specs=[SMEM] + [VMEM] * 3,
        out_specs=[VMEM] * 3,
        after=after,
    )(taps, g, from_high, from_low)


def finest_body(near, from_high, from_low, coarse, out):
    step = pl.program_id(0)
    at = 16 * step
    planes = [coarse[at + h] for h in range(19)]
    for k in range(32):
        h = k // 2
        value = planes[h + 1]
        if k % 2:
            value = 0.5625 * (value + planes[h + 2]) - 0.0625 * (planes[h] + planes[h + 3])
        value = value + near[32 * step + k]
        out[k, 0:8] = value[0:8] + from_low[32 * step + k]
        out[k, 8:120] = value[8:120]
        out[k, 120:128] = value[120:128] + from_high[32 * step + k]


def finest(near, from_high, from_low, coarse):
    return call(
        finest_body,
        [(64, 128, 128)],
        us=4,
        vmem=16,
        grid=(2,),
        in_specs=[VMEM] * 4,
        out_specs=[pl.BlockSpec((32, 128, 128), lambda i: (i, 0, 0))],
    )(near, from_high, from_low, coarse)[0]


def phi_at(dist):
    dist = jnp.abs(dist)
    return jnp.where(
        dist == 0, 1.0, jnp.where(dist == 1, 0.5625, jnp.where(dist == 3, -0.0625, 0.0))
    ).astype(F32)


def toeplitz(line, rows, offset):
    line = pltpu.roll(line, lax.rem(192 - offset, 128), 1)
    wide = jnp.broadcast_to(line[0:1], (rows, 128))
    return pltpu.roll(wide, 0, 1, stride=1, stride_axis=0)


def tables_body(taps, top_taps, rows1, rows2, ytab, ttab, ntab, tcoef, ncoef, oney, onex, edges):
    z, y, x = [lax.axis_index(name) for name in AXES]
    dist = jnp.abs(lane_of(8) - 64)
    line = jnp.zeros((8, 128), F32)
    for d in range(64):
        line = jnp.where(dist == d, top_taps[d], line)

    def inside(r, place, own, total):
        where = r + place * own
        return (where >= 0) & (where < total)

    def near(level, dist, keep):
        return jnp.where(keep, taps_at(taps, level, jnp.abs(dist)), 0.0)

    second = rows2[y]
    j, c = grid_of(128, 48)
    keep = (j < 64) & (c < 37) & inside(c - 2, y, 32, 128)
    right = jnp.where(keep, phi_at(y * 32 + c - 2 - 2 * j), 0.0).astype(BF16)
    for s in range(4):
        first = lax.rem(y + s, 4) * 16 - 2
        left = toeplitz(line, 24, -first)
        i, l = grid_of(24, 128)
        keep = (l < 64) & (i < 21) & (first + i >= 0) & (first + i < 64)
        full = exact_right(jnp.where(keep, left, 0.0), right)
        ytab[24 * s : 24 * s + 24, :] = exact_right(full, second)
    i, c = grid_of(72, 48)
    keep = (i < 37) & inside(i - 2, y, 32, 128)
    keep = keep | ((i >= 40) & (i < 53) & (y > 0)) | ((i >= 56) & (i < 69) & (y < 3))
    r = jnp.where(i < 40, i - 2, jnp.where(i < 56, i - 50, i - 26))
    ytab[96:168, :] = exact_right(near(2, r - (c - 2), keep), second)

    i, l = grid_of(128, 64)
    left = phi_at(x * 32 + i % 32 - 2 * l).astype(BF16)
    i, l = grid_of(64, 128)
    a, b = grid_of(128, 128)
    for s in range(4):
        first = lax.rem(x + s, 4) * 16 - 2
        right = toeplitz(line, 64, first)
        keep = (l < 21) & (first + l >= 0) & (first + l < 64)
        right = jnp.where(keep, right, 0.0)
        right = right + pltpu.roll(right, 32, 1)
        right = right + pltpu.roll(right, 64, 1)
        full = exact_left(left, right)
        ttab[:, 128 * s : 128 * s + 128] = jnp.where(a // 32 == b // 32, full, 0.0)
    i, l = grid_of(128, 256)
    r = l % 64 - 2
    keep = (l // 64 == i // 32) & (l % 64 < 37) & inside(r, x, 32, 128)
    ntab[:, 0:256] = near(2, r - i % 32, keep)
    i, l = grid_of(128, 128)
    same = l // 32 == i // 32
    ntab[:, 256:384] = near(2, l % 32 - 8 - i % 32, same & (l % 32 < 11) & (x > 0))
    ntab[:, 384:512] = near(2, l % 32 + 30 - i % 32, same & (l % 32 < 10) & (x < 3))

    i, l = grid_of(16, 64)
    left = phi_at(z * 16 + i - 2 * l).astype(BF16)
    i, l = grid_of(64, 128)
    parts = []
    for s in range(8):
        chip, core = lax.rem(z // 2 + s % 4, 4), lax.rem(z + s // 4, 2)
        first = (2 * chip + core) * 8 - 2
        right = toeplitz(line, 64, first)
        keep = (l < 13) & (first + l >= 0) & (first + l < 64)
        parts.append(exact_left(left, jnp.where(keep, right, 0.0)))
    whole = jnp.concatenate(parts, axis=0) * 0.125
    i, l = grid_of(128, 128)
    for quarter in range(4):
        spread = jnp.where(i == 4 * quarter + l // 32, 1.0, 0.0).astype(BF16)
        full = exact_right(whole, spread)
        for s in range(8):
            at = (s * 4 + quarter) * 16
            tcoef[at : at + 16, :] = full[16 * s : 16 * s + 16]
    i, l = grid_of(16, 128)
    g = l // 64
    for p in range(22):
        if p < 11:
            r = g + (2 * p - 2)
            keep = (r <= 18) & inside(r, z, 16, 128)
        elif p < 17:
            r = g + (2 * (p - 11) - 8)
            keep = (r <= 2) & (z > 0)
        else:
            r = g + (2 * (p - 17) + 14)
            keep = (r <= 23) & (z < 7)
        ncoef[16 * p : 16 * p + 16, :] = near(2, r - i, keep) * 0.25

    i, c = grid_of(104, 80)
    keep = (i < 67) & inside(i - 1, y, 64, 256)
    keep = keep | ((i >= 72) & (i < 83) & (y > 0)) | ((i >= 88) & (i < 99) & (y < 3))
    r = jnp.where(i < 72, i - 1, jnp.where(i < 88, i - 81, i - 25))
    oney[...] = exact_right(near(1, r - (c - 1), keep), rows1[y])
    i, l = grid_of(128, 256)
    r = l % 128 - 1
    keep = (l // 128 == i // 64) & (l % 128 < 67) & inside(r, x, 64, 256)
    onex[...] = near(1, r - i % 64, keep)
    i, l = grid_of(512, 128)
    same = l // 16 == i // 64
    edges[:, 0:128] = near(1, l % 16 - 8 - i % 64, same & (l % 16 < 10) & (x > 0))
    edges[:, 128:256] = near(1, l % 16 + 63 - i % 64, same & (l % 16 < 9) & (x < 3))


def tables(taps, top_taps, after):
    return call(
        tables_body,
        [
            (168, 128), (128, 512), (128, 512), (512, 128),
            (352, 128), (104, 128), (128, 256), (512, 256),
        ],
        us=2,
        in_specs=[SMEM, SMEM, VMEM, VMEM],
        out_specs=[VMEM] * 8,
        after=after,
    )(taps, top_taps, *[jnp.asarray(t) for t in chain_rows(512, 4)])


def rise_tables():
    def kron(table, groups):
        return np.stack([np.kron(np.eye(groups), t.T) for t in table])

    y2 = prolong_table(128, 4, 2, 3, 2, 3, (40, 24))
    x2 = kron(prolong_table(128, 4, 2, 3, 2, 3, (64, 32)), 4)
    y1 = prolong_table(256, 4, 1, 2, 2, 3, (72, 40))
    x1 = kron(prolong_table(256, 4, 1, 2, 2, 3, (128, 64)), 2)
    y0 = prolong_table(512, 4, 0, 0, 1, 2, (128, 72))
    x0 = kron(prolong_table(512, 4, 0, 0, 1, 2, (128, 128)), 1)
    mask2 = np.zeros((8, 11, 128), np.float32)
    mask1 = np.zeros((8, 35), np.float32)
    for place in range(8):
        for e in range(22):
            inside = 0 <= place * 16 - 2 + e < 128
            mask2[place, e // 2, 64 * (e % 2) : 64 * (e % 2) + 64] = inside
        for f in range(35):
            mask1[place, f] = 0 <= place * 32 - 1 + f < 256
    half = lambda table: jnp.asarray(table.astype(jnp.bfloat16))
    return half(y2), half(x2), jnp.asarray(mask2), half(y1), half(x1), jnp.asarray(mask1), half(y0), half(x0)


def per_device(charges, taps, top_taps):
    z, y, x = AXES
    chain = jnp.asarray(chain_tables(512, 4))

    one, two, low, high = coarse_z(charges)
    f_high, f_low = shift(low, z, -1), shift(high, z, 1)
    near, *nsides = near_z(taps, charges, (two,))
    nf_high, nf_low = shift(nsides[0], z, -1), shift(nsides[1], z, 1)
    ytab, ttab, ntab, tcoef, ncoef, oney, onex, edges = tables(taps, top_taps, (two,))

    one, two, low, high = coarse_x(chain, one, two, f_high, f_low, ())
    f_high, f_low = shift(low, x, -1), shift(high, x, 1)
    near, *nsides = near_x(taps, near, nf_high, nf_low, (two,))

    top, near2, near1, up, down, far, *nsides = top_y(ytab, oney, one, two, f_high, f_low, nsides)
    f_low, f_high, f_far = shift(up, y, 1), shift(down, y, -1), shift(far, y, 2)
    nf_high, nf_low = shift(nsides[0], x, -1), shift(nsides[1], x, 1)

    top, near2, near1, up, down, far = top_x(
        ttab, ntab, onex, edges, top, near2, near1, f_low, f_high, f_far, ()
    )
    f_low, f_high, f_far = shift(up, x, 1), shift(down, x, -1), shift(far, x, 2)
    near, *nsides = near_y(taps, near, nf_high, nf_low, (top,))

    top, partner, near2, near1, up, down = top_z(
        taps, tcoef, ncoef, top, near2, near1, f_low, f_high, f_far, (nsides[0],)
    )
    count = lax.axis_size(z)
    partner = lax.ppermute(partner, z, [(i, i ^ 1) for i in range(count)])
    f_low, f_high = shift(up, z, 1), shift(down, z, -1)
    nf_high, nf_low = shift(nsides[0], y, -1), shift(nsides[1], y, 1)
    top, *others = top_sum(top, partner, (nf_high, nf_low))
    others = [shift(part, z, 2 + 2 * k) for k, part in enumerate(others)]

    coarse = rise(rise_tables(), top, others, near2, f_low, f_high, near1)
    return finest(near, nf_high, nf_low, coarse)


def solution(mesh):
    return jax.shard_map(
        per_device,
        mesh=mesh,
        in_specs=(P("gz", "gy", "gx"), P(), P()),
        out_specs=P("gz", "gy", "gx"),
        check_vma=False,
    )
```
